32 devices in a mesh: grp: 2 (over y), site: 4 (over x, core), spin: 4 (over z).
Axes of the slice: x: 2, y: 2, z: 4, core: 2. Of those that a mesh axis runs over, the one named last changes fastest.
Arguments:
- walkers: bfloat16 [8, 512, 256, 256], P(('grp', 'spin'), 'site'), parts along dimension 0, may hold values from -90 to 90
- fields: bfloat16 [8, 1, 512, 256], P(('grp', 'spin'), None, 'site'), parts along dimension 0, may hold values from -3 to 3
- kinetic_x: bfloat16 [512, 512], replicated, may hold values from -0.5 to 1.5
- kinetic_y: bfloat16 [256, 256], replicated, may hold values from -0.5 to 1.5
Outputs:
- orthonormal: bfloat16 [8, 512, 256, 256], P(('grp', 'spin'), 'site'), parts along dimension 0
- triangle: float32 [8, 256, 256], P(('grp', 'spin')), parts along dimension 0
The draws below stay inside these ranges and needn't reach their ends.
There are 2 independent parts, one for each index of `grp`. The reference program is written for one: setup_inputs(seed, part) draws one part's arguments, and reference() takes and returns one part's arrays. A program takes and returns all parts, laid end to end along the dimension named above; an argument that names none is the same for every part. Nothing has to cross between parts.
All inputs are finite; a program needn't handle non-finite values.
Results may differ from the reference program's by a relative error of at most 0.0095.
Values may be sent and summed in bfloat16 or wider, within the bound.
No kernel may reach another device: no remote copies, remote signals or barrier semaphores. Data moves between devices by JAX's collectives and lax.ppermute only.
A program may use at most 128 MiB of HBM per device.

```python
import math
import jax
import jax.numpy as jnp
from jax import lax

LX = 512
LY = 256
ORBS = 256
STEPS = 1
SLOTS = 4


def kinetic_matrix(key, count):
    noise = jnp.clip(jax.random.normal(key, (count, count), jnp.float32), -6.0, 6.0)
    return (jnp.eye(count, dtype=jnp.float32) + 0.3 * noise / math.sqrt(count)).astype(jnp.bfloat16)


def draw_kinetic_x(key, part):
    return kinetic_matrix(jax.random.fold_in(key, 11), LX)


def draw_kinetic_y(key, part):
    return kinetic_matrix(jax.random.fold_in(key, 23), LY)


def draw_walkers(key, part):
    base_key, rough_key, column_key = jax.random.split(jax.random.fold_in(key, 37), 3)
    shape = (SLOTS, LX, LY, ORBS)
    base = jnp.clip(jax.random.normal(base_key, shape, jnp.float32), -6.0, 6.0)
    rise = jnp.exp(math.log(3.0) * jnp.arange(LX, dtype=jnp.float32) / (LX - 1))
    rough = jnp.exp(jax.random.uniform(rough_key, (SLOTS, LX, LY, 1), jnp.float32, 0.0, math.log(3.3)))
    columns = jnp.exp(jax.random.uniform(column_key, (SLOTS, 1, 1, ORBS), jnp.float32, math.log(0.3), math.log(3.0)))
    values = 0.5 * base * rise[None, :, None, None] * rough * columns
    return values.astype(jnp.bfloat16)


def level_of(own_key, extent, pieces, least, high):
    gain, own = 1.0, jax.random.fold_in(own_key, 6)
    for dim, shards_of in pieces:
        steps = jnp.exp(jax.random.uniform(jax.random.fold_in(own, dim), (shards_of,), jnp.float32, least / len(pieces), high / len(pieces)))
        gain = gain * jnp.repeat(steps, extent[dim] // shards_of).reshape([-1 if axis == dim else 1 for axis in range(len(extent))])
    return gain


def normal_values(key, dims, deviation, most, pieces=(), kind=jnp.bfloat16):
    array = jax.random.normal(key, dims, jnp.float32) * deviation
    if len(pieces) > 0:
        array = level_of(key, dims, pieces, -0.22, 0.18) * array
    return jnp.clip(array, min=-most, max=most).astype(kind)


def setup_inputs(seed: int = 0, part: int = 0) -> dict:
    keys = jax.random.split(jax.random.key(seed), 5)
    part_keys = jax.random.split(jax.random.fold_in(keys[4], part), 5)
    walkers = draw_walkers(jax.random.fold_in(jax.random.fold_in(keys[4], part), 71), part)
    fields = normal_values(part_keys[1], (SLOTS, STEPS, LX, LY), 0.4, 3.0, ((0, 4), (2, 4)))
    kinetic_x = draw_kinetic_x(jax.random.fold_in(keys[4], 71), part)
    kinetic_y = draw_kinetic_y(jax.random.fold_in(keys[4], 71), part)
    return dict(walkers=walkers, fields=fields, kinetic_x=kinetic_x, kinetic_y=kinetic_y)


def one_slot(walker, field, kinetic_x, kinetic_y):
    current = walker
    for step in range(STEPS):
        after_y = jnp.einsum('yz,xzm->xym', kinetic_y.astype(jnp.float32), current.astype(jnp.float32)).astype(jnp.bfloat16)
        flat_y = after_y.reshape(LX, LY * ORBS)
        after_x = jnp.dot(kinetic_x.astype(jnp.float32), flat_y.astype(jnp.float32), preferred_element_type=jnp.float32).astype(jnp.bfloat16).reshape(LX, LY, ORBS)
        factor = jnp.exp(field[step].astype(jnp.float32))
        current = (factor[:, :, None] * after_x.astype(jnp.float32)).astype(jnp.bfloat16)
    flat = current.reshape(LX * LY, ORBS)
    gram = jnp.dot(flat.T.astype(jnp.float32), flat.astype(jnp.float32), preferred_element_type=jnp.float32) * (1.0 / (LX * LY))
    lower = jnp.linalg.cholesky(gram)
    identity = jnp.eye(ORBS, dtype=jnp.float32)
    inverse = jax.scipy.linalg.solve_triangular(lower, identity, lower=True).T
    inverse_half = inverse.astype(jnp.bfloat16)
    result = jnp.dot(flat.astype(jnp.float32), inverse_half.astype(jnp.float32), preferred_element_type=jnp.float32).astype(jnp.bfloat16)
    return (result.reshape(LX, LY, ORBS), lower)

def reference(walkers, fields, kinetic_x, kinetic_y):

    def apply_one(pair):
        return one_slot(pair[0], pair[1], kinetic_x, kinetic_y)
    orthonormal, triangle = lax.map(apply_one, (walkers, fields))
    return (orthonormal, triangle)
```

```python
import functools

import jax
import jax.numpy as jnp
from jax import lax
from jax.experimental import pallas as pl
from jax.experimental.pallas import tpu as pltpu
from jax.sharding import PartitionSpec as P

ROWS = 16
LANES = 128
VMEM_LIMIT = 48 * 1024 * 1024


def partner(device, step, count):
    if count & (count - 1) == 0:
        return device ^ step
    return (step - device + count) % count


def trade(piece, step, count):
    if step == 0 and count & (count - 1) == 0:
        return piece
    return lax.ppermute(piece, "site", [(i, partner(i, step, count)) for i in range(count)])


def params():
    return pltpu.CompilerParams(vmem_limit_bytes=VMEM_LIMIT)


def y_kernel(count, chunks, band, part, walkers, kinetic, *rest):
    outs, own, turned = rest[:-2], rest[-2], rest[-1]
    me = lax.axis_index("site")
    depth = len(chunks) * count * part

    @pl.when(pl.program_id(0) == 0)
    def _():
        for i, c in enumerate(chunks):
            for s in range(count):
                start = pl.multiple_of(partner(me, s, count) * band + c * part, ROWS)
                own[pl.ds((i * count + s) * part, part), :] = kinetic[pl.ds(start, part), :]

    for r in range(ROWS):
        line = jnp.dot(own[...], walkers[r], preferred_element_type=jnp.float32)
        for h in range(turned.shape[0]):
            turned[h, pl.ds(r, depth, stride=ROWS), :] = line[:, h * LANES : (h + 1) * LANES]
    for k, out in enumerate(outs):
        for h in range(turned.shape[0]):
            piece = turned[h, pl.ds(k * part * ROWS, part * ROWS), :].astype(out.dtype)
            out[:, :, h * LANES : (h + 1) * LANES] = piece.reshape(part, ROWS, LANES)


def apply_y(walkers, kinetic_y, count, chunks, part):
    lines, width, orbitals = walkers.shape
    band = width // count
    pieces = len(chunks) * count
    depth = pieces * part
    return pl.pallas_call(
        functools.partial(y_kernel, count, chunks, band, part),
        grid=(lines // ROWS,),
        in_specs=[
            pl.BlockSpec((ROWS, width, orbitals), lambda i: (i, 0, 0)),
            pl.BlockSpec((width, width), lambda i: (0, 0)),
        ],
        out_specs=[pl.BlockSpec((part, ROWS, orbitals), lambda i: (0, i, 0))] * pieces,
        out_shape=[jax.ShapeDtypeStruct((part, lines, orbitals), jnp.bfloat16)] * pieces,
        scratch_shapes=[
            pltpu.VMEM((depth, width), jnp.bfloat16),
            pltpu.VMEM((orbitals // LANES, depth * ROWS, LANES), jnp.float32),
        ],
        compiler_params=params(),
        cost_estimate=pl.CostEstimate(
            flops=2 * depth * width * lines * orbitals,
            bytes_accessed=2 * lines * orbitals * (width + depth),
            transcendentals=0,
        ),
    )(walkers, kinetic_y)


def x_kernel(count, group, *refs):
    pieces, (field, kinetic, before) = refs[:count], refs[count : count + 3]
    outs, gram = refs[count + 3 : 2 * count + 3], refs[-1]

    @pl.when(pl.program_id(0) == 0)
    def _():
        gram[...] = before[...]

    factor = jnp.exp(field[0].astype(jnp.float32))
    total = jnp.zeros(gram.shape, jnp.float32)
    for j in range(group):
        lines = jnp.concatenate([piece[j] for piece in pieces], axis=0)
        moved = jnp.dot(kinetic[...], lines, preferred_element_type=jnp.float32)
        moved = moved.astype(jnp.bfloat16).astype(jnp.float32)
        scaled = (factor[:, j : j + 1] * moved).astype(jnp.bfloat16)
        block = scaled.shape[0] // count
        for t in range(count):
            outs[t][j] = scaled[t * block : (t + 1) * block]
        total += lax.dot_general(
            scaled, scaled, (((0,), (0,)), ((), ())), preferred_element_type=jnp.float32
        )
    gram[...] += total


def apply_x(pieces, fields, kinetic_x, gram):
    count = len(pieces)
    part, lines, orbitals = pieces[0].shape
    length = count * lines
    group = fields.shape[2]
    piece = pl.BlockSpec((group, lines, orbitals), lambda i: (i, 0, 0))
    square = pl.BlockSpec((orbitals, orbitals), lambda i: (0, 0))
    results = pl.pallas_call(
        functools.partial(x_kernel, count, group),
        grid=(part // group,),
        in_specs=[piece] * count
        + [
            pl.BlockSpec((1, length, group), lambda i: (i, 0, 0)),
            pl.BlockSpec((length, length), lambda i: (0, 0)),
            square,
        ],
        out_specs=[piece] * count + [square],
        out_shape=[jax.ShapeDtypeStruct(pieces[0].shape, jnp.bfloat16)] * count
        + [jax.ShapeDtypeStruct((orbitals, orbitals), jnp.float32)],
        compiler_params=params(),
        cost_estimate=pl.CostEstimate(
            flops=2 * part * length * orbitals * (length + orbitals),
            bytes_accessed=4 * part * length * orbitals,
            transcendentals=part * length,
        ),
    )(*pieces, fields, kinetic_x, gram)
    return results[:count], results[count]


def last_kernel(where, piece, inverse, *rest):
    out, turned = rest[-2], rest[-1]
    part, rows, orbitals = piece.shape
    product = jnp.dot(
        piece[...].reshape(part * rows, orbitals),
        inverse[...],
        preferred_element_type=jnp.float32,
    )
    for h in range(turned.shape[0]):
        turned[h] = product[:, h * LANES : (h + 1) * LANES]
        for r in range(rows):
            line = turned[h, pl.ds(r, part, stride=rows), :]
            out[r, :, h * LANES : (h + 1) * LANES] = line.astype(out.dtype)


def finish(result, piece, inverse, place, width):
    part, lines, orbitals = piece.shape
    begun = result is not None
    return pl.pallas_call(
        last_kernel,
        grid_spec=pltpu.PrefetchScalarGridSpec(
            num_scalar_prefetch=1,
            grid=(lines // ROWS,),
            in_specs=[
                pl.BlockSpec((part, ROWS, orbitals), lambda i, where: (0, i, 0)),
                pl.BlockSpec((orbitals, orbitals), lambda i, where: (0, 0)),
            ]
            + [pl.BlockSpec(memory_space=pl.ANY)] * begun,
            out_specs=pl.BlockSpec((ROWS, part, orbitals), lambda i, where: (i, where[0], 0)),
            scratch_shapes=[pltpu.VMEM((orbitals // LANES, part * ROWS, LANES), jnp.float32)],
        ),
        out_shape=jax.ShapeDtypeStruct((lines, width, orbitals), jnp.bfloat16),
        input_output_aliases={3: 0} if begun else {},
        compiler_params=params(),
        cost_estimate=pl.CostEstimate(
            flops=2 * part * lines * orbitals * orbitals,
            bytes_accessed=4 * part * lines * orbitals,
            transcendentals=0,
        ),
    )(place.reshape(1), piece, inverse, *([result] if begun else []))


def one_determinant(walkers, fields, kinetic_x, kinetic_y, count):
    lines, width, orbitals = walkers.shape
    me = lax.axis_index("site")
    band = width // count
    part = ROWS if band % ROWS == 0 else band
    chunks = band // part
    group = 8 if part % 8 == 0 else part
    steps = range(count)

    order = jnp.stack([partner(me, s, count) for s in steps])
    first = apply_y(walkers, kinetic_y, count, (0,), part)
    sent = [[trade(first[s], s, count) for s in steps]]
    if chunks > 1:
        more = apply_y(walkers, kinetic_y, count, tuple(range(1, chunks)), part)
        for c in range(1, chunks):
            sent.append([trade(more[(c - 1) * count + s], s, count) for s in steps])

    by_band = jnp.take(fields.reshape(lines, count, band), order, axis=1)
    own_fields = jnp.stack([trade(by_band[:, s], s, count) for s in steps])
    own_fields = own_fields.reshape(count * lines, band // group, group).swapaxes(0, 1)
    turned_x = kinetic_x.reshape(count, lines, count, lines)
    turned_x = jnp.take(jnp.take(turned_x, order, axis=0), order, axis=2).reshape(kinetic_x.shape)

    gram = jnp.zeros((orbitals, orbitals), jnp.float32)
    back = []
    per = part // group
    for c in range(chunks):
        pieces, gram = apply_x(sent[c], own_fields[c * per : (c + 1) * per], turned_x, gram)
        back.append([trade(pieces[s], s, count) for s in steps])

    gram = lax.psum(gram, "site") * (1.0 / (count * lines * width))
    lower = jnp.linalg.cholesky(gram)
    inverse = jax.scipy.linalg.solve_triangular(
        lower, jnp.eye(orbitals, dtype=jnp.float32), lower=True
    ).T.astype(jnp.bfloat16)

    result = None
    for c in range(chunks):
        for s in steps:
            result = finish(result, back[c][s], inverse, order[s] * chunks + c, width)
    return result, lower


def per_device(count, walkers, fields, kinetic_x, kinetic_y):
    results = [
        one_determinant(walkers[i], fields[i, 0], kinetic_x, kinetic_y, count)
        for i in range(walkers.shape[0])
    ]
    return tuple(jnp.stack(part) for part in zip(*results))


def solution(mesh):
    placed = (
        P(("grp", "spin"), "site", None, None),
        P(("grp", "spin"), None, "site", None),
        P(),
        P(),
    )
    return jax.shard_map(
        functools.partial(per_device, mesh.shape["site"]),
        mesh=mesh,
        in_specs=placed,
        out_specs=(P(("grp", "spin"), "site", None, None), P(("grp", "spin"), None, None)),
        check_vma=False,
    )
```

```python
import functools

import jax
import jax.numpy as jnp
from jax import lax
from jax.experimental import pallas as pl
from jax.experimental.pallas import tpu as pltpu
from jax.sharding import PartitionSpec as P

ROWS = 16
LANES = 128
BLOCK = 64
VMEM_LIMIT = 32 * 1024 * 1024
VMEM_MOST = 56 * 1024 * 1024


def partner(device, step, count):
    if count & (count - 1) == 0:
        return device ^ step
    return (step - device + count) % count


def trade(piece, step, count):
    if step == 0 and count & (count - 1) == 0:
        return piece
    return lax.ppermute(piece, "site", [(i, partner(i, step, count)) for i in range(count)])


def tie(*arrays):
    return lax.optimization_barrier(arrays)


def settings(limit=VMEM_LIMIT):
    return dict(
        compiler_params=pltpu.CompilerParams(vmem_limit_bytes=limit),
        cost_estimate=pl.CostEstimate(flops=1000, bytes_accessed=1000, transcendentals=0),
    )


def y_kernel(count, band, cuts, window, walkers, kinetic, *rest):
    outs, own, turned = rest[-2 - len(cuts) : -2], rest[-2], rest[-1]
    me = lax.axis_index("site")
    depth = own.shape[0]

    @pl.when(pl.program_id(0) == 0)
    def _():
        row = 0
        for s, first, size in cuts:
            start = pl.multiple_of(partner(me, s, count) * band + first, ROWS)
            own[pl.ds(row, size), :] = kinetic[pl.ds(start, size), :]
            row += size

    for r in range(ROWS):
        line = jnp.dot(own[...], walkers[r], preferred_element_type=jnp.float32)
        for h in range(turned.shape[0]):
            turned[h, pl.ds(r, depth, stride=ROWS), :] = line[:, h * LANES : (h + 1) * LANES]
    row = 0
    for (s, first, size), out in zip(cuts, outs):
        for h in range(turned.shape[0]):
            piece = turned[h, pl.ds(row * ROWS, size * ROWS), :].astype(out.dtype)
            out[:size, :, h * LANES : (h + 1) * LANES] = piece.reshape(size, ROWS, LANES)
        row += size
        if window:
            begin = pl.multiple_of(partner(me, s, count) * band // window * window, LANES)
            across = out.shape[2] // window
            for line in range(0, rest[0].shape[0], ROWS):
                place, part = size + line // ROWS // across, line // ROWS % across
                values = rest[0][pl.ds(line, ROWS), pl.ds(begin, window)]
                out[place, :, part * window : (part + 1) * window] = values


def apply_y(walkers, kinetic_y, count, cuts, sizes, fields=None, window=0):
    lines, width, orbitals = walkers.shape
    depth = sum(size for _, _, size in cuts)
    used = max(sizes)
    extra = fields.size // fields.shape[1] * window // (ROWS * orbitals) if window else 0

    def out_spec(cut, size):
        late = (used - size) // ROWS
        return pl.BlockSpec(
            (cut[2] + extra, ROWS, orbitals), lambda i: (0, jnp.maximum(i - late, 0) if late else i, 0)
        )

    return pl.pallas_call(
        functools.partial(y_kernel, count, width // count, cuts, window),
        grid=(used // ROWS,),
        in_specs=[
            pl.BlockSpec((ROWS, width, orbitals), lambda i: (i, 0, 0)),
            pl.BlockSpec((width, width), lambda i: (0, 0)),
        ]
        + [pl.BlockSpec((lines, width), lambda i: (0, 0))] * (window > 0),
        out_specs=[out_spec(cut, size) for cut, size in zip(cuts, sizes)],
        out_shape=[
            jax.ShapeDtypeStruct((cut[2] + extra, size, orbitals), jnp.bfloat16)
            for cut, size in zip(cuts, sizes)
        ],
        scratch_shapes=[
            pltpu.VMEM((depth, width), jnp.bfloat16),
            pltpu.VMEM((orbitals // LANES, depth * ROWS, LANES), jnp.float32),
        ],
        **settings(VMEM_MOST),
    )(walkers, kinetic_y, *([fields] if window else []))


def x_kernel(count, group, *refs):
    pieces, (field, kinetic, before) = refs[: -count - 4], refs[-count - 4 : -count - 1]
    outs, gram = refs[-count - 1 : -1], refs[-1]

    @pl.when(pl.program_id(0) == 0)
    def _():
        gram[...] = before[...]

    factor = jnp.exp(field[0].astype(jnp.float32))
    total = jnp.zeros(gram.shape, jnp.float32)
    for j in range(group):
        lines = jnp.concatenate([piece[j] for piece in pieces], axis=0)
        moved = jnp.dot(kinetic[...], lines, preferred_element_type=jnp.float32)
        moved = moved.astype(jnp.bfloat16).astype(jnp.float32)
        scaled = (factor[:, j : j + 1] * moved).astype(jnp.bfloat16)
        block = scaled.shape[0] // count
        for t in range(count):
            outs[t][j] = scaled[t * block : (t + 1) * block]
        total += lax.dot_general(
            scaled, scaled, (((0,), (0,)), ((), ())), preferred_element_type=jnp.float32
        )
    gram[...] += total


def apply_x(pieces, fields, kinetic_x, gram, count, first, part):
    orbitals = gram.shape[0]
    length = kinetic_x.shape[0]
    group = fields.shape[2]

    def spec(array, begin):
        offset = (first - begin) // group
        return pl.BlockSpec((group,) + array.shape[1:], lambda i: (i + offset, 0, 0))

    square = pl.BlockSpec((orbitals, orbitals), lambda i: (0, 0))
    out = (part, length // count, orbitals)
    results = pl.pallas_call(
        functools.partial(x_kernel, count, group),
        grid=(part // group,),
        in_specs=[spec(*piece) for piece in pieces]
        + [
            pl.BlockSpec((1, length, group), lambda i: (i + first // group, 0, 0)),
            pl.BlockSpec((length, length), lambda i: (0, 0)),
            square,
        ],
        out_specs=[pl.BlockSpec((group,) + out[1:], lambda i: (i, 0, 0))] * count + [square],
        out_shape=[jax.ShapeDtypeStruct(out, jnp.bfloat16)] * count
        + [jax.ShapeDtypeStruct((orbitals, orbitals), jnp.float32)],
        **settings(),
    )(*[array for array, _ in pieces], fields, kinetic_x, gram)
    return results[:count], results[count]


def last_kernel(where, piece, inverse, *rest):
    out, turned = rest[-2], rest[-1]
    part, rows, orbitals = piece.shape
    product = jnp.dot(
        piece[...].reshape(part * rows, orbitals),
        inverse[...],
        preferred_element_type=jnp.float32,
    )
    for h in range(turned.shape[0]):
        turned[h] = product[:, h * LANES : (h + 1) * LANES]
        for r in range(rows):
            line = turned[h, pl.ds(r, part, stride=rows), :]
            out[r, :, h * LANES : (h + 1) * LANES] = line.astype(out.dtype)


def finish(result, piece, inverse, place, width):
    part, lines, orbitals = piece.shape
    begun = result is not None
    rows = 4 * ROWS if lines % (4 * ROWS) == 0 else ROWS
    return pl.pallas_call(
        last_kernel,
        grid_spec=pltpu.PrefetchScalarGridSpec(
            num_scalar_prefetch=1,
            grid=(lines // rows,),
            in_specs=[
                pl.BlockSpec((part, rows, orbitals), lambda i, where: (0, i, 0)),
                pl.BlockSpec((orbitals, orbitals), lambda i, where: (0, 0)),
            ]
            + [pl.BlockSpec(memory_space=pl.ANY)] * begun,
            out_specs=pl.BlockSpec((rows, part, orbitals), lambda i, where: (i, where[0], 0)),
            scratch_shapes=[pltpu.VMEM((orbitals // LANES, part * rows, LANES), jnp.float32)],
        ),
        out_shape=jax.ShapeDtypeStruct((lines, width, orbitals), jnp.bfloat16),
        input_output_aliases={3: 0} if begun else {},
        **settings(),
    )(place.reshape(1), piece, inverse, *([result] if begun else []))


def factor_kernel(scale, gram, lower, inverse, work, upper):
    size = gram.shape[0]
    row = lax.broadcasted_iota(jnp.int32, (size, size), 0)
    column = lax.broadcasted_iota(jnp.int32, (size, size), 1)
    work[:, :size] = gram[...] * scale
    work[:, size:] = jnp.where(row == column, 1.0, 0.0)
    line = lax.broadcasted_iota(jnp.int32, (BLOCK, 2 * BLOCK), 0)
    lane = lax.broadcasted_iota(jnp.int32, (BLOCK, 2 * BLOCK), 1)
    identity = jnp.where(lane == line, 1.0, 0.0)[:, :BLOCK]
    dot = functools.partial(
        jnp.dot, precision=lax.Precision.HIGHEST, preferred_element_type=jnp.float32
    )
    for begin in range(0, size, BLOCK):
        end = begin + BLOCK
        both = jnp.concatenate([work[begin:end, begin:end], identity], axis=1)
        for j in range(BLOCK):
            pivot_column = jnp.broadcast_to(both[:, j : j + 1], both.shape)
            pivot = jnp.broadcast_to(pivot_column[j : j + 1], both.shape)
            root = lax.rsqrt(pivot)
            root = root * (1.5 - 0.5 * pivot * root * root)
            pivot_row = jnp.broadcast_to(both[j : j + 1], both.shape) * root
            below = both - pivot_column * root * pivot_row
            both = jnp.where(line > j, below, jnp.where(line == j, pivot_row, both))
        panel = dot(both[:, BLOCK:], work[begin:end, :])
        upper[begin:end, :] = panel[:, :size]
        work[begin:end, size:] = panel[:, size:]
        if end < size:
            work[end:, :] -= dot(panel[:, end:size].T, panel)
    lower[...] = jnp.where(row >= column, upper[...].T, 0.0)
    inverse[...] = work[:, size:].T.astype(inverse.dtype)


def factor(gram, scale):
    size = gram.shape[0]
    return pl.pallas_call(
        functools.partial(factor_kernel, scale),
        out_shape=[
            jax.ShapeDtypeStruct((size, size), jnp.float32),
            jax.ShapeDtypeStruct((size, size), jnp.bfloat16),
        ],
        scratch_shapes=[
            pltpu.VMEM((size, 2 * size), jnp.float32),
            pltpu.VMEM((size, size), jnp.float32),
        ],
        **settings(),
    )(gram)


def one_determinant(walkers, fields, kinetic_x, kinetic_y, count):
    lines, width, orbitals = walkers.shape
    me = lax.axis_index("site")
    band = width // count
    part = ROWS if band % ROWS == 0 else band
    group = 8 if part % 8 == 0 else part
    wide = 2 * part if band % (2 * part) == 0 else band
    steps = range(count)
    order = jnp.stack([partner(me, s, count) for s in steps])

    window = max(LANES, band)
    extra = lines * window // (ROWS * orbitals)
    far = [s for s in steps if s > 1 and lines > ROWS]
    near = [s for s in steps if s not in far]
    head = {}
    if far:
        arrays = apply_y(
            walkers, kinetic_y, count, [(s, 0, band) for s in far], [ROWS] * len(far), fields, window
        )
        kinetic_y, *arrays = tie(kinetic_y, *arrays)
        head = {s: trade(a, s, count) for s, a in zip(far, arrays)}
    cuts = [(s, first, wide) for first in range(0, band, wide) for s in far]
    cuts += [(s, 0, band) for s in near]
    sizes = [lines if s in near else lines - ROWS for s, _, _ in cuts]
    arrays = apply_y(walkers, kinetic_y, count, cuts, sizes)
    tail = {(s, first): a for (s, first, _), a in zip(cuts, arrays)}
    late = [key for key in tail if key[0] in near or key[1] > 0]
    if far:
        held = tie(*[tail[key] for key in late], *[head[s] for s in far])
        tail.update(zip(late, held))
        head.update(zip(far, held[len(late) :]))
    for s in far:
        tail[s, 0] = trade(tail[s, 0], s, count)
    for s in near:
        tail[s, 0] = trade(tail[s, 0], s, count)
    by_band = jnp.take(fields.reshape(lines, count, band), order, axis=1)
    by_band, tail[near[-1], 0] = tie(by_band, tail[near[-1], 0])
    own_fields = {s: trade(by_band[:, s], s, count) for s in near}
    for first in range(wide, band, wide):
        for s in far:
            if first > wide:
                tail[s, first], tail[s, first - 2 * wide] = tie(
                    tail[s, first], tail[s, first - 2 * wide]
                )
            elif s != far[0]:
                tail[s, first], tail[near[-1], 0] = tie(tail[s, first], tail[near[-1], 0])
            tail[s, first] = trade(tail[s, first], s, count)
    for s in far:
        sent = head[s][band:].reshape(extra, ROWS, orbitals // window, window)
        sent = jnp.swapaxes(sent, 1, 2).reshape(lines, window)
        own_fields[s] = lax.dynamic_slice_in_dim(sent, me * band % window, band, 1)
    own_fields = jnp.stack([own_fields[s] for s in steps])
    own_fields = own_fields.reshape(count * lines, band // group, group).swapaxes(0, 1)
    turned_x = kinetic_x.reshape(count, lines, count, lines)
    turned_x = jnp.take(jnp.take(turned_x, order, axis=0), order, axis=2).reshape(kinetic_x.shape)

    gram = jnp.zeros((orbitals, orbitals), jnp.float32)
    ready = []
    for first in range(0, band, part):
        pieces = []
        for s in steps:
            if s in far:
                pieces.append((head[s], 0))
            begin = first // wide * wide if s in far else 0
            pieces.append((tail[s, begin], begin))
        scaled, gram = apply_x(pieces, own_fields, turned_x, gram, count, first, part)
        ready.append(scaled)

    back = []
    half = orbitals // 2
    for c in range(min(2, len(ready))):
        back.append(dict(enumerate(ready[c])))
        for s in far:
            if c == 1 and (s, wide) in tail:
                back[c][s], tail[s, wide] = tie(back[c][s], tail[s, wide])
            back[c][s] = trade(back[c][s], s, count)
    if count & (count - 1) == 0 and count > 1:
        core = me & 1
        if far:
            gram, back[0][far[0]] = tie(gram, back[0][far[0]])
        mine = lax.dynamic_slice_in_dim(gram, core * half, half, 0)
        mine = mine + trade(lax.dynamic_slice_in_dim(gram, (1 - core) * half, half, 0), 1, count)
        for s in far[1:]:
            mine, back[0][s] = tie(mine, back[0][s])
        step = 2
        while step < count:
            mine = mine + trade(mine, step, count)
            step *= 2
        if len(back) > 1:
            for s in far:
                mine, back[1][s] = tie(mine, back[1][s])
        other = trade(mine, 1, count)
        gram = jnp.where(core == 0, jnp.concatenate([mine, other]), jnp.concatenate([other, mine]))
    else:
        gram = lax.psum(gram, "site")
    lower, inverse = factor(gram, 1.0 / (count * lines * width))

    for c in range(2, len(ready)):
        back.append(dict(enumerate(ready[c])))
        for s in far:
            if c == 2:
                back[c][s], back[0][s] = tie(back[c][s], back[0][s])
            else:
                back[c][s], inverse = tie(back[c][s], inverse)
            back[c][s] = trade(back[c][s], s, count)
    for c in range(len(back)):
        for s in near:
            back[c][s], gram = tie(back[c][s], gram)
            back[c][s] = trade(back[c][s], s, count)

    result = None
    for c in range(len(back)):
        for s in steps:
            place = order[s] * (band // part) + c
            result = finish(result, back[c][s], inverse, place, width)
    return result, lower


def per_device(count, walkers, fields, kinetic_x, kinetic_y):
    results = [
        one_determinant(walkers[i], fields[i, 0], kinetic_x, kinetic_y, count)
        for i in range(walkers.shape[0])
    ]
    return tuple(jnp.stack(part) for part in zip(*results))


def solution(mesh):
    placed = (
        P(("grp", "spin"), "site", None, None),
        P(("grp", "spin"), None, "site", None),
        P(),
        P(),
    )
    return jax.shard_map(
        functools.partial(per_device, mesh.shape["site"]),
        mesh=mesh,
        in_specs=placed,
        out_specs=(P(("grp", "spin"), "site", None, None), P(("grp", "spin"), None, None)),
        check_vma=False,
    )
```

```python
import functools

import jax
import jax.numpy as jnp
from jax import lax
from jax.experimental import pallas as pl
from jax.experimental.pallas import tpu as pltpu
from jax.sharding import PartitionSpec as P

ROWS = 16
LANES = 128
PAD = 8
BLOCK = 64
VMEM_LIMIT = 32 * 1024 * 1024
VMEM_MOST = 56 * 1024 * 1024


def partner(device, step, count):
    if count & (count - 1) == 0:
        return device ^ step
    return (step - device + count) % count


def trade(piece, step, count):
    if step == 0 and count & (count - 1) == 0:
        return piece
    return lax.ppermute(piece, "site", [(i, partner(i, step, count)) for i in range(count)])


def tie(*arrays):
    return lax.optimization_barrier(arrays)


def settings(limit=VMEM_LIMIT):
    return dict(
        compiler_params=pltpu.CompilerParams(vmem_limit_bytes=limit),
        cost_estimate=pl.CostEstimate(flops=1000, bytes_accessed=1000, transcendentals=0),
    )


def y_kernel(count, band, cuts, window, walkers, kinetic, *rest):
    outs, own, turned = rest[-2 - len(cuts) : -2], rest[-2], rest[-1]
    me = lax.axis_index("site")
    depth = own.shape[0]

    @pl.when(pl.program_id(0) == 0)
    def _():
        row = 0
        for s, first, size in cuts:
            start = pl.multiple_of(partner(me, s, count) * band + first, ROWS)
            own[pl.ds(row, size), :] = kinetic[pl.ds(start, size), :]
            row += size

    for r in range(ROWS):
        line = jnp.dot(own[...], walkers[r], preferred_element_type=jnp.float32)
        for h in range(turned.shape[0]):
            turned[h, pl.ds(r, depth, stride=ROWS + PAD), :] = line[:, h * LANES : (h + 1) * LANES]
    row = 0
    for (s, first, size), out in zip(cuts, outs):
        for h in range(turned.shape[0]):
            piece = turned[h, pl.ds(row * (ROWS + PAD), size * (ROWS + PAD)), :]
            piece = piece.reshape(size, ROWS + PAD, LANES)[:, :ROWS]
            out[:size, :, h * LANES : (h + 1) * LANES] = piece.astype(out.dtype)
        row += size
        if window:
            begin = pl.multiple_of(partner(me, s, count) * band // window * window, LANES)
            across = out.shape[2] // window
            for line in range(0, rest[0].shape[0], ROWS):
                place, part = size + line // ROWS // across, line // ROWS % across
                values = rest[0][pl.ds(line, ROWS), pl.ds(begin, window)]
                out[place, :, part * window : (part + 1) * window] = values


def apply_y(walkers, kinetic_y, count, cuts, sizes, fields=None, window=0):
    lines, width, orbitals = walkers.shape
    depth = sum(size for _, _, size in cuts)
    used = max(sizes)
    extra = fields.size // fields.shape[1] * window // (ROWS * orbitals) if window else 0

    def out_spec(cut, size):
        late = (used - size) // ROWS
        return pl.BlockSpec(
            (cut[2] + extra, ROWS, orbitals), lambda i: (0, jnp.maximum(i - late, 0) if late else i, 0)
        )

    return pl.pallas_call(
        functools.partial(y_kernel, count, width // count, cuts, window),
        grid=(used // ROWS,),
        in_specs=[
            pl.BlockSpec((ROWS, width, orbitals), lambda i: (i, 0, 0)),
            pl.BlockSpec((width, width), lambda i: (0, 0)),
        ]
        + [pl.BlockSpec((lines, width), lambda i: (0, 0))] * (window > 0),
        out_specs=[out_spec(cut, size) for cut, size in zip(cuts, sizes)],
        out_shape=[
            jax.ShapeDtypeStruct((cut[2] + extra, size, orbitals), jnp.bfloat16)
            for cut, size in zip(cuts, sizes)
        ],
        scratch_shapes=[
            pltpu.VMEM((depth, width), jnp.bfloat16),
            pltpu.VMEM((orbitals // LANES, depth * (ROWS + PAD), LANES), jnp.float32),
        ],
        **settings(VMEM_MOST),
    )(walkers, kinetic_y, *([fields] if window else []))


def x_kernel(count, group, *refs):
    pieces, (field, kinetic, before) = refs[: -count - 4], refs[-count - 4 : -count - 1]
    outs, gram = refs[-count - 1 : -1], refs[-1]

    @pl.when(pl.program_id(0) == 0)
    def _():
        gram[...] = before[...]

    factor = jnp.exp(field[0].astype(jnp.float32))
    total = jnp.zeros(gram.shape, jnp.float32)
    for j in range(group):
        lines = jnp.concatenate([piece[j] for piece in pieces], axis=0)
        moved = jnp.dot(kinetic[...], lines, preferred_element_type=jnp.float32)
        moved = moved.astype(jnp.bfloat16).astype(jnp.float32)
        scaled = (factor[:, j : j + 1] * moved).astype(jnp.bfloat16)
        block = scaled.shape[0] // count
        for t in range(count):
            outs[t][j] = scaled[t * block : (t + 1) * block]
        total += lax.dot_general(
            scaled, scaled, (((0,), (0,)), ((), ())), preferred_element_type=jnp.float32
        )
    gram[...] += total


def apply_x(pieces, fields, kinetic_x, gram, count, first, part):
    orbitals = gram.shape[0]
    length = kinetic_x.shape[0]
    group = fields.shape[2]

    def spec(array, begin):
        offset = (first - begin) // group
        return pl.BlockSpec((group,) + array.shape[1:], lambda i: (i + offset, 0, 0))

    square = pl.BlockSpec((orbitals, orbitals), lambda i: (0, 0))
    out = (part, length // count, orbitals)
    results = pl.pallas_call(
        functools.partial(x_kernel, count, group),
        grid=(part // group,),
        in_specs=[spec(*piece) for piece in pieces]
        + [
            pl.BlockSpec((1, length, group), lambda i: (i + first // group, 0, 0)),
            pl.BlockSpec((length, length), lambda i: (0, 0)),
            square,
        ],
        out_specs=[pl.BlockSpec((group,) + out[1:], lambda i: (i, 0, 0))] * count + [square],
        out_shape=[jax.ShapeDtypeStruct(out, jnp.bfloat16)] * count
        + [jax.ShapeDtypeStruct((orbitals, orbitals), jnp.float32)],
        **settings(),
    )(*[array for array, _ in pieces], fields, kinetic_x, gram)
    return results[:count], results[count]


def last_kernel(where, piece, inverse, *rest):
    out, turned = rest[-2], rest[-1]
    part, rows, orbitals = piece.shape
    product = jnp.dot(
        piece[...].reshape(part * rows, orbitals),
        inverse[...],
        preferred_element_type=jnp.float32,
    )
    for h in range(turned.shape[0]):
        for y in range(part):
            lines = product[y * rows : (y + 1) * rows, h * LANES : (h + 1) * LANES]
            turned[h, pl.ds(y * (rows + PAD), rows), :] = lines
        for r in range(rows):
            line = turned[h, pl.ds(r, part, stride=rows + PAD), :]
            out[r, :, h * LANES : (h + 1) * LANES] = line.astype(out.dtype)


def finish(result, piece, inverse, place, width):
    part, lines, orbitals = piece.shape
    begun = result is not None
    rows = 4 * ROWS if lines % (4 * ROWS) == 0 else ROWS
    return pl.pallas_call(
        last_kernel,
        grid_spec=pltpu.PrefetchScalarGridSpec(
            num_scalar_prefetch=1,
            grid=(lines // rows,),
            in_specs=[
                pl.BlockSpec((part, rows, orbitals), lambda i, where: (0, i, 0)),
                pl.BlockSpec((orbitals, orbitals), lambda i, where: (0, 0)),
            ]
            + [pl.BlockSpec(memory_space=pl.ANY)] * begun,
            out_specs=pl.BlockSpec((rows, part, orbitals), lambda i, where: (i, where[0], 0)),
            scratch_shapes=[pltpu.VMEM((orbitals // LANES, part * (rows + PAD), LANES), jnp.float32)],
        ),
        out_shape=jax.ShapeDtypeStruct((lines, width, orbitals), jnp.bfloat16),
        input_output_aliases={3: 0} if begun else {},
        **settings(),
    )(place.reshape(1), piece, inverse, *([result] if begun else []))


def factor_kernel(scale, gram, lower, inverse, work, upper):
    size = gram.shape[0]
    row = lax.broadcasted_iota(jnp.int32, (size, size), 0)
    column = lax.broadcasted_iota(jnp.int32, (size, size), 1)
    work[:, :size] = gram[...] * scale
    work[:, size:] = jnp.where(row == column, 1.0, 0.0)
    line = lax.broadcasted_iota(jnp.int32, (BLOCK, 2 * BLOCK), 0)
    lane = lax.broadcasted_iota(jnp.int32, (BLOCK, 2 * BLOCK), 1)
    identity = jnp.where(lane == line, 1.0, 0.0)[:, :BLOCK]
    dot = functools.partial(
        jnp.dot, precision=lax.Precision.HIGHEST, preferred_element_type=jnp.float32
    )
    for begin in range(0, size, BLOCK):
        end = begin + BLOCK
        both = jnp.concatenate([work[begin:end, begin:end], identity], axis=1)
        for j in range(BLOCK):
            pivot_column = jnp.broadcast_to(both[:, j : j + 1], both.shape)
            pivot = jnp.broadcast_to(pivot_column[j : j + 1], both.shape)
            root = lax.rsqrt(pivot)
            root = root * (1.5 - 0.5 * pivot * root * root)
            pivot_row = jnp.broadcast_to(both[j : j + 1], both.shape) * root
            below = both - pivot_column * root * pivot_row
            both = jnp.where(line > j, below, jnp.where(line == j, pivot_row, both))
        panel = dot(both[:, BLOCK:], work[begin:end, :])
        upper[begin:end, :] = panel[:, :size]
        work[begin:end, size:] = panel[:, size:]
        if end < size:
            work[end:, :] -= dot(panel[:, end:size].T, panel)
    lower[...] = jnp.where(row >= column, upper[...].T, 0.0)
    inverse[...] = work[:, size:].T.astype(inverse.dtype)


def factor(gram, scale):
    size = gram.shape[0]
    return pl.pallas_call(
        functools.partial(factor_kernel, scale),
        out_shape=[
            jax.ShapeDtypeStruct((size, size), jnp.float32),
            jax.ShapeDtypeStruct((size, size), jnp.bfloat16),
        ],
        scratch_shapes=[
            pltpu.VMEM((size, 2 * size), jnp.float32),
            pltpu.VMEM((size, size), jnp.float32),
        ],
        **settings(),
    )(gram)


def one_determinant(walkers, fields, kinetic_x, kinetic_y, count):
    lines, width, orbitals = walkers.shape
    me = lax.axis_index("site")
    band = width // count
    part = ROWS if band % ROWS == 0 else band
    group = 8 if part % 8 == 0 else part
    wide = 2 * part if band % (2 * part) == 0 else band
    steps = range(count)
    order = jnp.stack([partner(me, s, count) for s in steps])

    window = max(LANES, band)
    extra = lines * window // (ROWS * orbitals)
    far = [s for s in steps if s > 1 and lines > ROWS]
    near = [s for s in steps if s not in far]
    head = {}
    if far:
        arrays = apply_y(
            walkers, kinetic_y, count, [(s, 0, band) for s in far], [ROWS] * len(far), fields, window
        )
        kinetic_y, *arrays = tie(kinetic_y, *arrays)
        head = {s: trade(a, s, count) for s, a in zip(far, arrays)}
    cuts = [(s, first, wide) for first in range(0, band, wide) for s in far]
    cuts += [(s, 0, band) for s in near]
    sizes = [lines if s in near else lines - ROWS for s, _, _ in cuts]
    arrays = apply_y(walkers, kinetic_y, count, cuts, sizes)
    tail = {(s, first): a for (s, first, _), a in zip(cuts, arrays)}
    late = [key for key in tail if key[0] in near or key[1] > 0]
    if far:
        held = tie(*[tail[key] for key in late], *[head[s] for s in far])
        tail.update(zip(late, held))
        head.update(zip(far, held[len(late) :]))
    for s in far:
        tail[s, 0] = trade(tail[s, 0], s, count)
    for s in near:
        tail[s, 0] = trade(tail[s, 0], s, count)
    by_band = jnp.take(fields.reshape(lines, count, band), order, axis=1)
    by_band, tail[near[-1], 0] = tie(by_band, tail[near[-1], 0])
    own_fields = {s: trade(by_band[:, s], s, count) for s in near}
    for first in range(wide, band, wide):
        for s in far:
            if first > wide:
                tail[s, first], tail[s, first - 2 * wide] = tie(
                    tail[s, first], tail[s, first - 2 * wide]
                )
            elif s != far[0]:
                tail[s, first], tail[near[-1], 0] = tie(tail[s, first], tail[near[-1], 0])
            tail[s, first] = trade(tail[s, first], s, count)
    for s in far:
        sent = head[s][band:].reshape(extra, ROWS, orbitals // window, window)
        sent = jnp.swapaxes(sent, 1, 2).reshape(lines, window)
        own_fields[s] = lax.dynamic_slice_in_dim(sent, me * band % window, band, 1)
    own_fields = jnp.stack([own_fields[s] for s in steps])
    own_fields = own_fields.reshape(count * lines, band // group, group).swapaxes(0, 1)
    turned_x = kinetic_x.reshape(count, lines, count, lines)
    turned_x = jnp.take(jnp.take(turned_x, order, axis=0), order, axis=2).reshape(kinetic_x.shape)

    gram = jnp.zeros((orbitals, orbitals), jnp.float32)
    ready = []
    for first in range(0, band, part):
        pieces = []
        for s in steps:
            if s in far:
                pieces.append((head[s], 0))
            begin = first // wide * wide if s in far else 0
            pieces.append((tail[s, begin], begin))
        scaled, gram = apply_x(pieces, own_fields, turned_x, gram, count, first, part)
        ready.append(scaled)

    back = []
    half = orbitals // 2
    for c in range(min(2, len(ready))):
        back.append(dict(enumerate(ready[c])))
        for s in far:
            if c == 1 and (s, wide) in tail:
                back[c][s], tail[s, wide] = tie(back[c][s], tail[s, wide])
            if c == 1 and s != far[0]:
                back[c][s], back[0][far[-1]] = tie(back[c][s], back[0][far[-1]])
            back[c][s] = trade(back[c][s], s, count)
    if count & (count - 1) == 0 and count > 1:
        core = me & 1
        if far:
            gram, back[0][far[0]] = tie(gram, back[0][far[0]])
        mine = lax.dynamic_slice_in_dim(gram, core * half, half, 0)
        mine = mine + trade(lax.dynamic_slice_in_dim(gram, (1 - core) * half, half, 0), 1, count)
        step = 2
        while step < count:
            mine = mine + trade(mine, step, count)
            step *= 2
        if len(back) > 1 and far:
            mine, back[1][far[0]] = tie(mine, back[1][far[0]])
        other = trade(mine, 1, count)
        gram = jnp.where(core == 0, jnp.concatenate([mine, other]), jnp.concatenate([other, mine]))
    else:
        gram = lax.psum(gram, "site")
    lower, inverse = factor(gram, 1.0 / (count * lines * width))

    for c in range(2, len(ready)):
        back.append(dict(enumerate(ready[c])))
        for s in far:
            if c == 2:
                back[c][s], back[0][s] = tie(back[c][s], back[0][s])
            else:
                back[c][s], inverse = tie(back[c][s], inverse)
            back[c][s] = trade(back[c][s], s, count)
    for c in range(len(back)):
        for s in near:
            back[c][s], gram = tie(back[c][s], gram)
            back[c][s] = trade(back[c][s], s, count)

    result = None
    for c in range(len(back)):
        for s in steps:
            place = order[s] * (band // part) + c
            result = finish(result, back[c][s], inverse, place, width)
    return result, lower


def per_device(count, walkers, fields, kinetic_x, kinetic_y):
    results = [
        one_determinant(walkers[i], fields[i, 0], kinetic_x, kinetic_y, count)
        for i in range(walkers.shape[0])
    ]
    return tuple(jnp.stack(part) for part in zip(*results))


def solution(mesh):
    placed = (
        P(("grp", "spin"), "site", None, None),
        P(("grp", "spin"), None, "site", None),
        P(),
        P(),
    )
    return jax.shard_map(
        functools.partial(per_device, mesh.shape["site"]),
        mesh=mesh,
        in_specs=placed,
        out_specs=(P(("grp", "spin"), "site", None, None), P(("grp", "spin"), None, None)),
        check_vma=False,
    )
```

```python
import functools

import jax
import jax.numpy as jnp
from jax import lax
from jax.experimental import pallas as pl
from jax.experimental.pallas import tpu as pltpu
from jax.sharding import PartitionSpec as P

ROWS = 16
LANES = 128
PAD = 8
BLOCK = 64
VMEM_LIMIT = 20 * 1024 * 1024
VMEM_LEAST = 8 * 1024 * 1024
VMEM_MOST = 56 * 1024 * 1024


def partner(device, step, count):
    if count & (count - 1) == 0:
        return device ^ step
    return (step - device + count) % count


def trade(piece, step, count):
    if step == 0 and count & (count - 1) == 0:
        return piece
    return lax.ppermute(piece, "site", [(i, partner(i, step, count)) for i in range(count)])


def tie(*arrays):
    return lax.optimization_barrier(arrays)


def settings(limit=VMEM_LIMIT):
    return dict(
        compiler_params=pltpu.CompilerParams(vmem_limit_bytes=limit),
        cost_estimate=pl.CostEstimate(flops=1000, bytes_accessed=1000, transcendentals=0),
    )


def y_kernel(count, band, cuts, window, walkers, kinetic, *rest):
    outs, own, turned = rest[-2 - len(cuts) : -2], rest[-2], rest[-1]
    me = lax.axis_index("site")
    depth = own.shape[0]

    @pl.when(pl.program_id(0) == 0)
    def _():
        row = 0
        for s, first, size in cuts:
            start = pl.multiple_of(partner(me, s, count) * band + first, ROWS)
            own[pl.ds(row, size), :] = kinetic[pl.ds(start, size), :]
            row += size

    fine = walkers.shape[0]
    turn = pl.program_id(0) % (ROWS // fine)
    for r in range(fine):
        line = jnp.dot(own[...], walkers[r], preferred_element_type=jnp.float32)
        at = turn * fine + r if fine < ROWS else r
        for h in range(turned.shape[0]):
            part = line[:, h * LANES : (h + 1) * LANES]
            turned[h, pl.ds(at, depth, stride=ROWS + PAD), :] = part
    if fine < ROWS:
        pl.when(turn == ROWS // fine - 1)(functools.partial(write_cuts, count, band, cuts, window, outs, turned, rest))
    else:
        write_cuts(count, band, cuts, window, outs, turned, rest)


def write_cuts(count, band, cuts, window, outs, turned, rest):
    me = lax.axis_index("site")
    row = 0
    for (s, first, size), out in zip(cuts, outs):
        for h in range(turned.shape[0]):
            piece = turned[h, pl.ds(row * (ROWS + PAD), size * (ROWS + PAD)), :]
            piece = piece.reshape(size, ROWS + PAD, LANES)[:, :ROWS]
            out[:size, :, h * LANES : (h + 1) * LANES] = piece.astype(out.dtype)
        row += size
        if window:
            begin = partner(me, s, count) * band
            tile = pl.multiple_of(begin // window * window, LANES)
            across = out.shape[2] // band
            for line in range(0, rest[0].shape[0], ROWS):
                place, part = size + line // ROWS // across, line // ROWS % across
                values = rest[0][pl.ds(line, ROWS), pl.ds(tile, window)].astype(jnp.float32)
                own_values = values[:, :band]
                for k in range(band, window, band):
                    own_values = jnp.where(begin - tile == k, values[:, k : k + band], own_values)
                out[place, :, part * band : (part + 1) * band] = own_values.astype(out.dtype)


def rows_for_fields(lines, band, orbitals):
    return -(-lines * band // (ROWS * orbitals))


def apply_y(walkers, kinetic_y, count, cuts, sizes, fine, fields=None, window=0):
    lines, width, orbitals = walkers.shape
    depth = sum(size for _, _, size in cuts)
    used = max(sizes)
    extra = rows_for_fields(lines, width // count, orbitals) if window else 0

    def out_spec(cut, size):
        late = (used - size) // ROWS
        return pl.BlockSpec(
            (cut[2] + extra, ROWS, orbitals), lambda i: (0, jnp.maximum(i * fine // ROWS - late, 0), 0)
        )

    return pl.pallas_call(
        functools.partial(y_kernel, count, width // count, cuts, window),
        grid=(used // fine,),
        in_specs=[
            pl.BlockSpec((fine, width, orbitals), lambda i: (i, 0, 0)),
            pl.BlockSpec((width, width), lambda i: (0, 0)),
        ]
        + [pl.BlockSpec((lines, width), lambda i: (0, 0))] * (window > 0),
        out_specs=[out_spec(cut, size) for cut, size in zip(cuts, sizes)],
        out_shape=[
            jax.ShapeDtypeStruct((cut[2] + extra, size, orbitals), jnp.bfloat16)
            for cut, size in zip(cuts, sizes)
        ],
        scratch_shapes=[
            pltpu.VMEM((depth, width), jnp.bfloat16),
            pltpu.VMEM((orbitals // LANES, depth * (ROWS + PAD), LANES), jnp.float32),
        ],
        **settings(VMEM_MOST),
    )(walkers, kinetic_y, *([fields] if window else []))


def x_kernel(count, group, *refs):
    pieces, (field, kinetic, before) = refs[: -count - 4], refs[-count - 4 : -count - 1]
    outs, gram = refs[-count - 1 : -1], refs[-1]

    @pl.when(pl.program_id(0) == 0)
    def _():
        gram[...] = before[...]

    factor = jnp.exp(field[0].astype(jnp.float32))
    total = jnp.zeros(gram.shape, jnp.float32)
    for j in range(group):
        lines = jnp.concatenate([piece[j] for piece in pieces], axis=0)
        moved = jnp.dot(kinetic[...], lines, preferred_element_type=jnp.float32)
        moved = moved.astype(jnp.bfloat16).astype(jnp.float32)
        scaled = (factor[:, j : j + 1] * moved).astype(jnp.bfloat16)
        block = scaled.shape[0] // count
        for t in range(count):
            outs[t][j] = scaled[t * block : (t + 1) * block]
        total += lax.dot_general(
            scaled, scaled, (((0,), (0,)), ((), ())), preferred_element_type=jnp.float32
        )
    gram[...] += total


def apply_x(pieces, fields, kinetic_x, gram, count, first, part):
    orbitals = gram.shape[0]
    length = kinetic_x.shape[0]
    group = fields.shape[2]

    def spec(array, begin):
        offset = (first - begin) // group
        return pl.BlockSpec((group,) + array.shape[1:], lambda i: (i + offset, 0, 0))

    square = pl.BlockSpec((orbitals, orbitals), lambda i: (0, 0))
    out = (part, length // count, orbitals)
    results = pl.pallas_call(
        functools.partial(x_kernel, count, group),
        grid=(part // group,),
        in_specs=[spec(*piece) for piece in pieces]
        + [
            pl.BlockSpec((1, length, group), lambda i: (i + first // group, 0, 0)),
            pl.BlockSpec((length, length), lambda i: (0, 0)),
            square,
        ],
        out_specs=[pl.BlockSpec((group,) + out[1:], lambda i: (i, 0, 0))] * count + [square],
        out_shape=[jax.ShapeDtypeStruct(out, jnp.bfloat16)] * count
        + [jax.ShapeDtypeStruct((orbitals, orbitals), jnp.float32)],
        **settings(),
    )(*[array for array, _ in pieces], fields, kinetic_x, gram)
    return results[:count], results[count]


def times_inverse(piece, inverse, turned, out):
    part, rows, _ = piece.shape
    product = jnp.dot(
        piece[...].reshape(part * rows, piece.shape[2]),
        inverse[...],
        preferred_element_type=jnp.float32,
    )
    for h in range(turned.shape[0]):
        for y in range(part):
            lines = product[y * rows : (y + 1) * rows, h * LANES : (h + 1) * LANES]
            turned[h, pl.ds(y * (rows + PAD), rows), :] = lines
        for r in range(rows):
            line = turned[h, pl.ds(r, part, stride=rows + PAD), :]
            out[r, :, h * LANES : (h + 1) * LANES] = line.astype(out.dtype)


def last_kernel(where, piece, inverse, *rest):
    times_inverse(piece, inverse, rest[-1], rest[-2])


def split_kernel(piece, inverse, *rest):
    for k, out in enumerate(rest[:-1]):
        pl.when(pl.program_id(0) == k)(
            functools.partial(times_inverse, piece, inverse, rest[-1], out)
        )


def place_kernel(where, piece, result, out):
    out[...] = piece[...]


def split(piece, inverse):
    part, lines, orbitals = piece.shape
    rows = 4 * ROWS if lines % (4 * ROWS) == 0 else lines
    out = (rows, part, orbitals)
    return pl.pallas_call(
        split_kernel,
        grid=(lines // rows,),
        in_specs=[
            pl.BlockSpec((part, rows, orbitals), lambda i: (0, i, 0)),
            pl.BlockSpec((orbitals, orbitals), lambda i: (0, 0)),
        ],
        out_specs=[pl.BlockSpec(out, lambda i: (0, 0, 0))] * (lines // rows),
        out_shape=[jax.ShapeDtypeStruct(out, jnp.bfloat16)] * (lines // rows),
        scratch_shapes=[pltpu.VMEM((orbitals // LANES, part * (rows + PAD), LANES), jnp.float32)],
        **settings(VMEM_LEAST),
    )(piece, inverse)


def place(result, piece, begin, where):
    lines, part, orbitals = piece.shape
    rows = lines // 2 if begin % (lines // 2) == 0 else lines
    block = (rows, part, orbitals)
    return pl.pallas_call(
        place_kernel,
        grid_spec=pltpu.PrefetchScalarGridSpec(
            num_scalar_prefetch=1,
            grid=(lines // rows,),
            in_specs=[
                pl.BlockSpec(block, lambda i, where: (i, 0, 0)),
                pl.BlockSpec(memory_space=pl.ANY),
            ],
            out_specs=pl.BlockSpec(block, lambda i, where: (begin // rows + i, where[0], 0)),
        ),
        out_shape=jax.ShapeDtypeStruct(result.shape, result.dtype),
        input_output_aliases={2: 0},
        **settings(VMEM_LEAST),
    )(where.reshape(1), piece, result)


def finish(result, piece, inverse, place, width):
    part, lines, orbitals = piece.shape
    begun = result is not None
    rows = 4 * ROWS if lines % (4 * ROWS) == 0 else ROWS
    return pl.pallas_call(
        last_kernel,
        grid_spec=pltpu.PrefetchScalarGridSpec(
            num_scalar_prefetch=1,
            grid=(lines // rows,),
            in_specs=[
                pl.BlockSpec((part, rows, orbitals), lambda i, where: (0, i, 0)),
                pl.BlockSpec((orbitals, orbitals), lambda i, where: (0, 0)),
            ]
            + [pl.BlockSpec(memory_space=pl.ANY)] * begun,
            out_specs=pl.BlockSpec((rows, part, orbitals), lambda i, where: (i, where[0], 0)),
            scratch_shapes=[pltpu.VMEM((orbitals // LANES, part * (rows + PAD), LANES), jnp.float32)],
        ),
        out_shape=jax.ShapeDtypeStruct((lines, width, orbitals), jnp.bfloat16),
        input_output_aliases={3: 0} if begun else {},
        **settings(VMEM_LEAST),
    )(place.reshape(1), piece, inverse, *([result] if begun else []))


def factor_kernel(scale, first, second, lower, inverse, work, upper):
    size = lower.shape[0]
    quarter = size // 4
    upper[3 * quarter :, :] = first[:, :size]
    upper[:quarter, :quarter] = first[:, size:]
    upper[2 * quarter : 3 * quarter, : 3 * quarter] = second[:, : 3 * quarter]
    upper[quarter : 2 * quarter, : 2 * quarter] = second[:, 3 * quarter :]
    row = lax.broadcasted_iota(jnp.int32, (size, size), 0)
    column = lax.broadcasted_iota(jnp.int32, (size, size), 1)
    work[:, :size] = jnp.where(row >= column, upper[...], upper[...].T) * scale
    work[:, size:] = jnp.where(row == column, 1.0, 0.0)
    line = lax.broadcasted_iota(jnp.int32, (BLOCK, 2 * BLOCK), 0)
    lane = lax.broadcasted_iota(jnp.int32, (BLOCK, 2 * BLOCK), 1)
    identity = jnp.where(lane == line, 1.0, 0.0)[:, :BLOCK]
    dot = functools.partial(
        jnp.dot, precision=lax.Precision.HIGHEST, preferred_element_type=jnp.float32
    )
    for begin in range(0, size, BLOCK):
        end = begin + BLOCK
        both = jnp.concatenate([work[begin:end, begin:end], identity], axis=1)
        for j in range(BLOCK):
            pivot_column = jnp.broadcast_to(both[:, j : j + 1], both.shape)
            pivot = jnp.broadcast_to(pivot_column[j : j + 1], both.shape)
            root = lax.rsqrt(pivot)
            root = root * (1.5 - 0.5 * pivot * root * root)
            pivot_row = jnp.broadcast_to(both[j : j + 1], both.shape) * root
            below = both - pivot_column * root * pivot_row
            both = jnp.where(line > j, below, jnp.where(line == j, pivot_row, both))
        panel = dot(both[:, BLOCK:], work[begin:end, :])
        upper[begin:end, :] = panel[:, :size]
        work[begin:end, size:] = panel[:, size:]
        if end < size:
            work[end:, :] -= dot(panel[:, end:size].T, panel)
    lower[...] = jnp.where(row >= column, upper[...].T, 0.0)
    inverse[...] = work[:, size:].T.astype(inverse.dtype)


def pack(gram):
    quarter = gram.shape[0] // 4
    first = [gram[3 * quarter :], gram[:quarter, :quarter]]
    second = [gram[2 * quarter : 3 * quarter, : 3 * quarter], gram[quarter : 2 * quarter, : 2 * quarter]]
    return jnp.concatenate(first, axis=1), jnp.concatenate(second, axis=1)


def factor(first, second, scale):
    size = first.shape[0] * 4
    return pl.pallas_call(
        functools.partial(factor_kernel, scale),
        out_shape=[
            jax.ShapeDtypeStruct((size, size), jnp.float32),
            jax.ShapeDtypeStruct((size, size), jnp.bfloat16),
        ],
        scratch_shapes=[
            pltpu.VMEM((size, 2 * size), jnp.float32),
            pltpu.VMEM((size, size), jnp.float32),
        ],
        **settings(VMEM_LEAST),
    )(first, second)


def one_determinant(walkers, fields, kinetic_x, kinetic_y, count):
    lines, width, orbitals = walkers.shape
    me = lax.axis_index("site")
    band = width // count
    part = ROWS if band % ROWS == 0 else band
    chunks = band // part
    group = 8 if part % 8 == 0 else part
    wide = 2 * part if band % (2 * part) == 0 else band
    steps = range(count)
    order = jnp.stack([partner(me, s, count) for s in steps])

    window = max(LANES, band)
    extra = rows_for_fields(lines, band, orbitals)
    far = [s for s in steps if s > 1 and lines > ROWS]
    near = [s for s in steps if s not in far]
    head = {}
    if far:
        arrays = apply_y(
            walkers, kinetic_y, count, [(s, 0, band) for s in far], [ROWS] * len(far), ROWS, fields, window
        )
        kinetic_y, *arrays = tie(kinetic_y, *arrays)
        head = {s: trade(a, s, count) for s, a in zip(far, arrays)}
    cuts = [(s, first, wide) for first in range(0, band, wide) for s in far]
    cuts += [(s, 0, band) for s in near]
    sizes = [lines if s in near else lines - ROWS for s, _, _ in cuts]
    arrays = apply_y(walkers, kinetic_y, count, cuts, sizes, ROWS)
    tail = {(s, first): a for (s, first, _), a in zip(cuts, arrays)}
    late = [key for key in tail if key[0] in near or key[1] > 0]
    if far:
        held = tie(*[tail[key] for key in late], *[head[s] for s in far])
        tail.update(zip(late, held))
        head.update(zip(far, held[len(late) :]))
    for s in far:
        tail[s, 0] = trade(tail[s, 0], s, count)
    for s in near:
        tail[s, 0] = trade(tail[s, 0], s, count)
    by_band = jnp.take(fields.reshape(lines, count, band), order, axis=1)
    by_band, tail[near[-1], 0] = tie(by_band, tail[near[-1], 0])
    own_fields = {s: trade(by_band[:, s], s, count) for s in near}
    for first in range(wide, band, wide):
        for s in far:
            if first > wide:
                tail[s, first], tail[s, first - 2 * wide] = tie(
                    tail[s, first], tail[s, first - 2 * wide]
                )
            elif s != far[0]:
                tail[s, first], tail[near[-1], 0] = tie(tail[s, first], tail[near[-1], 0])
            tail[s, first] = trade(tail[s, first], s, count)
    for s in far:
        sent = head[s][band:].reshape(extra, ROWS, orbitals // band, band)
        own_fields[s] = jnp.swapaxes(sent, 1, 2).reshape(-1, band)[:lines]
    own_fields = jnp.stack([own_fields[s] for s in steps])
    own_fields = own_fields.reshape(count * lines, band // group, group).swapaxes(0, 1)
    turned_x = kinetic_x.reshape(count, lines, count, lines)
    turned_x = jnp.take(jnp.take(turned_x, order, axis=0), order, axis=2).reshape(kinetic_x.shape)

    gram = jnp.zeros((orbitals, orbitals), jnp.float32)
    ready = []
    for first in range(0, band, part):
        pieces = []
        for s in steps:
            if s in far:
                pieces.append((head[s], 0))
            begin = first // wide * wide if s in far else 0
            pieces.append((tail[s, begin], begin))
        scaled, gram = apply_x(pieces, own_fields, turned_x, gram, count, first, part)
        ready.append(scaled)

    back = []
    for c in range(min(2, len(ready))):
        back.append(dict(enumerate(ready[c])))
        for s in far:
            if c == 1 and (s, wide) in tail:
                back[c][s], tail[s, wide] = tie(back[c][s], tail[s, wide])
            if c == 1 and s != far[0]:
                back[c][s], back[0][far[-1]] = tie(back[c][s], back[0][far[-1]])
            back[c][s] = trade(back[c][s], s, count)
    if count & (count - 1) == 0 and count > 1:
        core = me & 1
        if far:
            gram, back[0][far[0]] = tie(gram, back[0][far[0]])
        first, second = pack(gram)
        mine = jnp.where(core == 0, first, second)
        mine = mine + trade(jnp.where(core == 0, second, first), 1, count)
        step = 2
        while step < count:
            mine = mine + trade(mine, step, count)
            step *= 2
        if len(back) > 1 and far:
            mine, back[1][far[0]] = tie(mine, back[1][far[0]])
        other = trade(mine, 1, count)
        first, second = jnp.where(core == 0, mine, other), jnp.where(core == 0, other, mine)
    else:
        first, second = pack(lax.psum(gram, "site"))
    lower, inverse = factor(first, second, 1.0 / (count * lines * width))

    for c in range(2, len(ready)):
        back.append(dict(enumerate(ready[c])))
        for s in far:
            if c == 2:
                back[c][s], back[0][s] = tie(back[c][s], back[0][s])
            elif c < chunks - 1:
                back[c][s], inverse = tie(back[c][s], inverse)
            if 2 < c == chunks - 1:
                back[c][s] = [trade(piece, s, count) for piece in split(back[c][s], inverse)]
            else:
                back[c][s] = trade(back[c][s], s, count)
    for c in range(len(back)):
        for s in near:
            back[c][s], first = tie(back[c][s], first)
            back[c][s] = trade(back[c][s], s, count)

    result = None
    for c in range(chunks):
        for s in steps:
            if not isinstance(back[c][s], list):
                where = order[s] * chunks + c
                result = finish(result, back[c][s], inverse, where, width)
    for s in far:
        if isinstance(back[-1][s], list):
            pieces = back[-1][s]
            for k, piece in enumerate(pieces):
                where = order[s] * chunks + chunks - 1
                result = place(result, piece, k * piece.shape[0], where)
    return result, lower


def per_device(count, walkers, fields, kinetic_x, kinetic_y):
    results = [
        one_determinant(walkers[i], fields[i, 0], kinetic_x, kinetic_y, count)
        for i in range(walkers.shape[0])
    ]
    return tuple(jnp.stack(part) for part in zip(*results))


def solution(mesh):
    placed = (
        P(("grp", "spin"), "site", None, None),
        P(("grp", "spin"), None, "site", None),
        P(),
        P(),
    )
    return jax.shard_map(
        functools.partial(per_device, mesh.shape["site"]),
        mesh=mesh,
        in_specs=placed,
        out_specs=(P(("grp", "spin"), "site", None, None), P(("grp", "spin"), None, None)),
        check_vma=False,
    )
```

```python
import functools

import jax
import jax.numpy as jnp
from jax import lax
from jax.experimental import pallas as pl
from jax.experimental.pallas import tpu as pltpu
from jax.sharding import PartitionSpec as P

ROWS = 16
LANES = 128
PAD = 8
BLOCK = 64
VMEM_LIMIT = 20 * 1024 * 1024
VMEM_LEAST = 8 * 1024 * 1024
VMEM_MOST = 56 * 1024 * 1024


def partner(device, step, count):
    if count & (count - 1) == 0:
        return device ^ step
    return (step - device + count) % count


def trade(piece, step, count):
    if step == 0 and count & (count - 1) == 0:
        return piece
    return lax.ppermute(piece, "site", [(i, partner(i, step, count)) for i in range(count)])


def tie(*arrays):
    return lax.optimization_barrier(arrays)


def settings(limit=VMEM_LIMIT):
    return dict(
        compiler_params=pltpu.CompilerParams(vmem_limit_bytes=limit),
        cost_estimate=pl.CostEstimate(flops=1000, bytes_accessed=1000, transcendentals=0),
    )


def y_kernel(count, band, cuts, carry, walkers, kinetic, *rest):
    outs, own, turned = rest[-2 - len(cuts) : -2], rest[-2], rest[-1]
    me = lax.axis_index("site")
    depth = own.shape[0]

    @pl.when(pl.program_id(0) == 0)
    def _():
        row = 0
        for s, first, size in cuts:
            start = pl.multiple_of(partner(me, s, count) * band + first, ROWS)
            own[pl.ds(row, size), :] = kinetic[pl.ds(start, size), :]
            row += size

    for r in range(ROWS):
        line = jnp.dot(own[...], walkers[r], preferred_element_type=jnp.float32)
        for h in range(turned.shape[0]):
            part = line[:, h * LANES : (h + 1) * LANES]
            turned[h, pl.ds(r, depth, stride=ROWS + PAD), :] = part
    row = 0
    for (s, first, size), out in zip(cuts, outs):
        for h in range(turned.shape[0]):
            piece = turned[h, pl.ds(row * (ROWS + PAD), size * (ROWS + PAD)), :]
            piece = piece.reshape(size, ROWS + PAD, LANES)[:, :ROWS]
            out[:size, :, h * LANES : (h + 1) * LANES] = piece.astype(out.dtype)
        row += size
        if s in carry and first == 0:
            window = max(LANES, band)
            begin = partner(me, s, count) * band
            tile = pl.multiple_of(begin // window * window, LANES)
            across = out.shape[2] // band
            for line in range(0, rest[0].shape[0], ROWS):
                place, part = size + line // ROWS // across, line // ROWS % across
                values = rest[0][pl.ds(line, ROWS), pl.ds(tile, window)].astype(jnp.float32)
                own_values = values[:, :band]
                for k in range(band, window, band):
                    own_values = jnp.where(begin - tile == k, values[:, k : k + band], own_values)
                out[place, :, part * band : (part + 1) * band] = own_values.astype(out.dtype)


def rows_for_fields(lines, band, orbitals):
    return -(-lines * band // (ROWS * orbitals))


def apply_y(walkers, kinetic_y, fields, count, cuts, sizes, carry):
    lines, width, orbitals = walkers.shape
    depth = sum(size for _, _, size in cuts)
    used = max(sizes)
    extra = rows_for_fields(lines, width // count, orbitals)

    def out_rows(cut):
        return cut[2] + (extra if cut[0] in carry and cut[1] == 0 else 0)

    def out_spec(cut, size):
        late = (used - size) // ROWS
        return pl.BlockSpec(
            (out_rows(cut), ROWS, orbitals),
            lambda i: (0, jnp.maximum(i - late, 0) if late else i, 0),
        )

    return pl.pallas_call(
        functools.partial(y_kernel, count, width // count, cuts, carry),
        grid=(used // ROWS,),
        in_specs=[
            pl.BlockSpec((ROWS, width, orbitals), lambda i: (i, 0, 0)),
            pl.BlockSpec((width, width), lambda i: (0, 0)),
            pl.BlockSpec((lines, width), lambda i: (0, 0)),
        ],
        out_specs=[out_spec(cut, size) for cut, size in zip(cuts, sizes)],
        out_shape=[
            jax.ShapeDtypeStruct((out_rows(cut), size, orbitals), jnp.bfloat16)
            for cut, size in zip(cuts, sizes)
        ],
        scratch_shapes=[
            pltpu.VMEM((depth, width), jnp.bfloat16),
            pltpu.VMEM((orbitals // LANES, depth * (ROWS + PAD), LANES), jnp.float32),
        ],
        **settings(VMEM_MOST),
    )(walkers, kinetic_y, fields)


def x_kernel(count, group, *refs):
    pieces, (field, kinetic, before) = refs[: -count - 4], refs[-count - 4 : -count - 1]
    outs, gram = refs[-count - 1 : -1], refs[-1]

    @pl.when(pl.program_id(0) == 0)
    def _():
        gram[...] = before[...]

    factor = jnp.exp(field[0].astype(jnp.float32))
    total = jnp.zeros(gram.shape, jnp.float32)
    for j in range(group):
        lines = jnp.concatenate([piece[j] for piece in pieces], axis=0)
        moved = jnp.dot(kinetic[...], lines, preferred_element_type=jnp.float32)
        moved = moved.astype(jnp.bfloat16).astype(jnp.float32)
        scaled = (factor[:, j : j + 1] * moved).astype(jnp.bfloat16)
        block = scaled.shape[0] // count
        for t in range(count):
            outs[t][j] = scaled[t * block : (t + 1) * block]
        total += lax.dot_general(
            scaled, scaled, (((0,), (0,)), ((), ())), preferred_element_type=jnp.float32
        )
    gram[...] += total


def apply_x(pieces, fields, kinetic_x, gram, count, first, part):
    orbitals = gram.shape[0]
    length = kinetic_x.shape[0]
    group = fields.shape[2]

    def spec(array, begin):
        offset = (first - begin) // group
        return pl.BlockSpec((group,) + array.shape[1:], lambda i: (i + offset, 0, 0))

    square = pl.BlockSpec((orbitals, orbitals), lambda i: (0, 0))
    out = (part, length // count, orbitals)
    results = pl.pallas_call(
        functools.partial(x_kernel, count, group),
        grid=(part // group,),
        in_specs=[spec(*piece) for piece in pieces]
        + [
            pl.BlockSpec((1, length, group), lambda i: (i + first // group, 0, 0)),
            pl.BlockSpec((length, length), lambda i: (0, 0)),
            square,
        ],
        out_specs=[pl.BlockSpec((group,) + out[1:], lambda i: (i, 0, 0))] * count + [square],
        out_shape=[jax.ShapeDtypeStruct(out, jnp.bfloat16)] * count
        + [jax.ShapeDtypeStruct((orbitals, orbitals), jnp.float32)],
        **settings(),
    )(*[array for array, _ in pieces], fields, kinetic_x, gram)
    return results[:count], results[count]


def times_inverse(piece, inverse, turned, out):
    part, rows, _ = piece.shape
    product = jnp.dot(
        piece[...].reshape(part * rows, piece.shape[2]),
        inverse[...],
        preferred_element_type=jnp.float32,
    )
    for h in range(turned.shape[0]):
        for y in range(part):
            lines = product[y * rows : (y + 1) * rows, h * LANES : (h + 1) * LANES]
            turned[h, pl.ds(y * (rows + PAD), rows), :] = lines
        for r in range(rows):
            line = turned[h, pl.ds(r, part, stride=rows + PAD), :]
            out[r, :, h * LANES : (h + 1) * LANES] = line.astype(out.dtype)


def last_kernel(where, piece, inverse, *rest):
    times_inverse(piece, inverse, rest[-1], rest[-2])


def split_kernel(piece, inverse, *rest):
    for k, out in enumerate(rest[:-1]):
        pl.when(pl.program_id(0) == k)(
            functools.partial(times_inverse, piece, inverse, rest[-1], out)
        )


def place_kernel(where, piece, result, out):
    out[...] = piece[...]


def split(piece, inverse):
    part, lines, orbitals = piece.shape
    rows = 4 * ROWS if lines % (4 * ROWS) == 0 else lines
    out = (rows, part, orbitals)
    return pl.pallas_call(
        split_kernel,
        grid=(lines // rows,),
        in_specs=[
            pl.BlockSpec((part, rows, orbitals), lambda i: (0, i, 0)),
            pl.BlockSpec((orbitals, orbitals), lambda i: (0, 0)),
        ],
        out_specs=[pl.BlockSpec(out, lambda i: (0, 0, 0))] * (lines // rows),
        out_shape=[jax.ShapeDtypeStruct(out, jnp.bfloat16)] * (lines // rows),
        scratch_shapes=[pltpu.VMEM((orbitals // LANES, part * (rows + PAD), LANES), jnp.float32)],
        **settings(VMEM_LEAST),
    )(piece, inverse)


def place(result, piece, begin, where):
    lines, part, orbitals = piece.shape
    rows = lines // 2 if begin % (lines // 2) == 0 else lines
    block = (rows, part, orbitals)
    return pl.pallas_call(
        place_kernel,
        grid_spec=pltpu.PrefetchScalarGridSpec(
            num_scalar_prefetch=1,
            grid=(lines // rows,),
            in_specs=[
                pl.BlockSpec(block, lambda i, where: (i, 0, 0)),
                pl.BlockSpec(memory_space=pl.ANY),
            ],
            out_specs=pl.BlockSpec(block, lambda i, where: (begin // rows + i, where[0], 0)),
        ),
        out_shape=jax.ShapeDtypeStruct(result.shape, result.dtype),
        input_output_aliases={2: 0},
        **settings(VMEM_LEAST),
    )(where.reshape(1), piece, result)


def finish(result, piece, inverse, place, width):
    part, lines, orbitals = piece.shape
    begun = result is not None
    rows = 4 * ROWS if lines % (4 * ROWS) == 0 else ROWS
    return pl.pallas_call(
        last_kernel,
        grid_spec=pltpu.PrefetchScalarGridSpec(
            num_scalar_prefetch=1,
            grid=(lines // rows,),
            in_specs=[
                pl.BlockSpec((part, rows, orbitals), lambda i, where: (0, i, 0)),
                pl.BlockSpec((orbitals, orbitals), lambda i, where: (0, 0)),
            ]
            + [pl.BlockSpec(memory_space=pl.ANY)] * begun,
            out_specs=pl.BlockSpec((rows, part, orbitals), lambda i, where: (i, where[0], 0)),
            scratch_shapes=[pltpu.VMEM((orbitals // LANES, part * (rows + PAD), LANES), jnp.float32)],
        ),
        out_shape=jax.ShapeDtypeStruct((lines, width, orbitals), jnp.bfloat16),
        input_output_aliases={3: 0} if begun else {},
        **settings(VMEM_LEAST),
    )(place.reshape(1), piece, inverse, *([result] if begun else []))


def factor_kernel(scale, first, second, lower, inverse, work, upper):
    size = lower.shape[0]
    quarter = size // 4
    upper[3 * quarter :, :] = first[:, :size]
    upper[:quarter, :quarter] = first[:, size:]
    upper[2 * quarter : 3 * quarter, : 3 * quarter] = second[:, : 3 * quarter]
    upper[quarter : 2 * quarter, : 2 * quarter] = second[:, 3 * quarter :]
    row = lax.broadcasted_iota(jnp.int32, (size, size), 0)
    column = lax.broadcasted_iota(jnp.int32, (size, size), 1)
    work[:, :size] = jnp.where(row >= column, upper[...], upper[...].T) * scale
    work[:, size:] = jnp.where(row == column, 1.0, 0.0)
    line = lax.broadcasted_iota(jnp.int32, (BLOCK, 2 * BLOCK), 0)
    lane = lax.broadcasted_iota(jnp.int32, (BLOCK, 2 * BLOCK), 1)
    identity = jnp.where(lane == line, 1.0, 0.0)[:, :BLOCK]
    dot = functools.partial(
        jnp.dot, precision=lax.Precision.HIGHEST, preferred_element_type=jnp.float32
    )
    for begin in range(0, size, BLOCK):
        end = begin + BLOCK
        both = jnp.concatenate([work[begin:end, begin:end], identity], axis=1)
        for j in range(BLOCK):
            pivot_column = jnp.broadcast_to(both[:, j : j + 1], both.shape)
            pivot = jnp.broadcast_to(pivot_column[j : j + 1], both.shape)
            root = lax.rsqrt(pivot)
            root = root * (1.5 - 0.5 * pivot * root * root)
            pivot_row = jnp.broadcast_to(both[j : j + 1], both.shape) * root
            below = both - pivot_column * root * pivot_row
            both = jnp.where(line > j, below, jnp.where(line == j, pivot_row, both))
        panel = dot(both[:, BLOCK:], work[begin:end, :])
        upper[begin:end, :] = panel[:, :size]
        work[begin:end, size:] = panel[:, size:]
        if end < size:
            work[end:, :] -= dot(panel[:, end:size].T, panel)
    lower[...] = jnp.where(row >= column, upper[...].T, 0.0)
    inverse[...] = work[:, size:].T.astype(inverse.dtype)


def pack(gram):
    quarter = gram.shape[0] // 4
    first = [gram[3 * quarter :], gram[:quarter, :quarter]]
    second = [gram[2 * quarter : 3 * quarter, : 3 * quarter], gram[quarter : 2 * quarter, : 2 * quarter]]
    return jnp.concatenate(first, axis=1), jnp.concatenate(second, axis=1)


def factor(first, second, scale):
    size = first.shape[0] * 4
    return pl.pallas_call(
        functools.partial(factor_kernel, scale),
        out_shape=[
            jax.ShapeDtypeStruct((size, size), jnp.float32),
            jax.ShapeDtypeStruct((size, size), jnp.bfloat16),
        ],
        scratch_shapes=[
            pltpu.VMEM((size, 2 * size), jnp.float32),
            pltpu.VMEM((size, size), jnp.float32),
        ],
        **settings(VMEM_LEAST),
    )(first, second)


def one_determinant(walkers, fields, kinetic_x, kinetic_y, count):
    lines, width, orbitals = walkers.shape
    me = lax.axis_index("site")
    band = width // count
    part = ROWS if band % ROWS == 0 else band
    chunks = band // part
    group = 8 if part % 8 == 0 else part
    wide = 2 * part if band % (2 * part) == 0 else band
    steps = range(count)
    order = jnp.stack([partner(me, s, count) for s in steps])

    extra = rows_for_fields(lines, band, orbitals)
    far = [s for s in steps if s > 1 and lines > ROWS]
    near = [s for s in steps if s not in far]
    head = {}
    if far:
        cuts = [(s, 0, band) for s in far]
        arrays = apply_y(walkers, kinetic_y, fields, count, cuts, [ROWS] * len(far), far)
        kinetic_y, *arrays = tie(kinetic_y, *arrays)
        head = {s: trade(a, s, count) for s, a in zip(far, arrays)}
    near_cuts = [(0, part), (part, part), (2 * part, band - 2 * part)] if chunks >= 4 else [(0, band)]
    cuts = [(s, first, wide) for first in range(0, band, wide) for s in far]
    cuts += [(s, *cut) for s in near for cut in ([(0, band)] if s == 0 or not far else near_cuts)]
    sizes = [lines if s in near else lines - ROWS for s, _, _ in cuts]
    arrays = apply_y(walkers, kinetic_y, fields, count, cuts, sizes, near)
    tail = {(s, first): a for (s, first, _), a in zip(cuts, arrays)}
    def hold(key, *keys):
        held = tie(tail[key], *[tail[k] if isinstance(k, tuple) else head[k] for k in keys])
        tail[key] = held[0]
        for k, array in zip(keys, held[1:]):
            (tail if isinstance(k, tuple) else head)[k] = array

    sent = set()

    def go(key):
        tail[key] = trade(tail[key], key[0], count)
        sent.add(key)

    for s in far:
        go((s, 0))
    if far and chunks >= 4:
        y, z = (near[-1], 0), (near[-1], part)
        hold(y, *far)
        go(y)
        hold(z, y, *[(s, 0) for s in far])
        go(z)
    for key in tail:
        if key not in sent:
            go(key)
    own_fields = []
    for s in steps:
        sent = (head[s] if s in far else tail[s, 0])[-extra:, :ROWS]
        sent = sent.reshape(extra, ROWS, orbitals // band, band)
        own_fields.append(jnp.swapaxes(sent, 1, 2).reshape(-1, band)[:lines])
    own_fields = jnp.stack(own_fields)
    own_fields = own_fields.reshape(count * lines, band // group, group).swapaxes(0, 1)
    turned_x = kinetic_x.reshape(count, lines, count, lines)
    turned_x = jnp.take(jnp.take(turned_x, order, axis=0), order, axis=2).reshape(kinetic_x.shape)

    gram = jnp.zeros((orbitals, orbitals), jnp.float32)
    ready = []
    for first in range(0, band, part):
        pieces = []
        for s in steps:
            if s in far:
                pieces.append((head[s], 0))
            begin = max(at for step, at in tail if step == s and at <= first)
            pieces.append((tail[s, begin], begin))
        scaled, gram = apply_x(pieces, own_fields, turned_x, gram, count, first, part)
        ready.append(scaled)

    back = []
    for c in range(min(2, len(ready))):
        back.append(dict(enumerate(ready[c])))
        for s in far:
            if c == 1 and (s, wide) in tail:
                back[c][s], tail[s, wide] = tie(back[c][s], tail[s, wide])
            if c == 1 and s != far[0]:
                back[c][s], back[0][far[-1]] = tie(back[c][s], back[0][far[-1]])
            back[c][s] = trade(back[c][s], s, count)
    if count & (count - 1) == 0 and count > 1:
        core = me & 1
        if far:
            gram, back[0][far[0]] = tie(gram, back[0][far[0]])
        first, second = pack(gram)
        mine = jnp.where(core == 0, first, second)
        mine = mine + trade(jnp.where(core == 0, second, first), 1, count)
        step = 2
        while step < count:
            mine = mine + trade(mine, step, count)
            step *= 2
        if len(back) > 1 and far:
            mine, back[1][far[0]] = tie(mine, back[1][far[0]])
        other = trade(mine, 1, count)
        first, second = jnp.where(core == 0, mine, other), jnp.where(core == 0, other, mine)
    else:
        first, second = pack(lax.psum(gram, "site"))
    lower, inverse = factor(first, second, 1.0 / (count * lines * width))

    for c in range(2, len(ready)):
        back.append(dict(enumerate(ready[c])))
        for s in far:
            if c == 2:
                back[c][s], back[0][s] = tie(back[c][s], back[0][s])
            elif c < chunks - 1:
                back[c][s], inverse = tie(back[c][s], inverse)
            if 2 < c == chunks - 1:
                back[c][s] = [trade(piece, s, count) for piece in split(back[c][s], inverse)]
            else:
                back[c][s] = trade(back[c][s], s, count)
    for c in range(len(back)):
        for s in near:
            back[c][s], first = tie(back[c][s], first)
            back[c][s] = trade(back[c][s], s, count)

    result = None
    for c in range(chunks):
        for s in steps:
            if not isinstance(back[c][s], list):
                where = order[s] * chunks + c
                result = finish(result, back[c][s], inverse, where, width)
    for s in far:
        if isinstance(back[-1][s], list):
            pieces = back[-1][s]
            for k, piece in enumerate(pieces):
                where = order[s] * chunks + chunks - 1
                result = place(result, piece, k * piece.shape[0], where)
    return result, lower


def per_device(count, walkers, fields, kinetic_x, kinetic_y):
    results = [
        one_determinant(walkers[i], fields[i, 0], kinetic_x, kinetic_y, count)
        for i in range(walkers.shape[0])
    ]
    return tuple(jnp.stack(part) for part in zip(*results))


def solution(mesh):
    placed = (
        P(("grp", "spin"), "site", None, None),
        P(("grp", "spin"), None, "site", None),
        P(),
        P(),
    )
    return jax.shard_map(
        functools.partial(per_device, mesh.shape["site"]),
        mesh=mesh,
        in_specs=placed,
        out_specs=(P(("grp", "spin"), "site", None, None), P(("grp", "spin"), None, None)),
        check_vma=False,
    )
```

```python
import functools

import jax
import jax.numpy as jnp
from jax import lax
from jax.experimental import pallas as pl
from jax.experimental.pallas import tpu as pltpu
from jax.sharding import PartitionSpec as P

ROWS = 16
LANES = 128
PAD = 8
BLOCK = 64
VMEM_LIMIT = 20 * 1024 * 1024
VMEM_LEAST = 8 * 1024 * 1024
VMEM_MOST = 56 * 1024 * 1024


def partner(device, step, count):
    if count & (count - 1) == 0:
        return device ^ step
    return (step - device + count) % count


def trade(piece, step, count):
    if step == 0 and count & (count - 1) == 0:
        return piece
    return lax.ppermute(piece, "site", [(i, partner(i, step, count)) for i in range(count)])


def tie(*arrays):
    return lax.optimization_barrier(arrays)


def settings(limit=VMEM_LIMIT):
    return dict(
        compiler_params=pltpu.CompilerParams(vmem_limit_bytes=limit),
        cost_estimate=pl.CostEstimate(flops=1000, bytes_accessed=1000, transcendentals=0),
    )


def y_kernel(count, band, cuts, carry, walkers, kinetic, *rest):
    outs, own, turned = rest[-2 - len(cuts) : -2], rest[-2], rest[-1]
    me = lax.axis_index("site")
    depth = own.shape[0]

    @pl.when(pl.program_id(0) == 0)
    def _():
        row = 0
        for s, first, size in cuts:
            start = pl.multiple_of(partner(me, s, count) * band + first, ROWS)
            own[pl.ds(row, size), :] = kinetic[pl.ds(start, size), :]
            row += size

    for r in range(ROWS):
        line = jnp.dot(own[...], walkers[r], preferred_element_type=jnp.float32)
        for h in range(turned.shape[0]):
            part = line[:, h * LANES : (h + 1) * LANES]
            turned[h, pl.ds(r, depth, stride=ROWS + PAD), :] = part
    row = 0
    for (s, first, size), out in zip(cuts, outs):
        for h in range(turned.shape[0]):
            piece = turned[h, pl.ds(row * (ROWS + PAD), size * (ROWS + PAD)), :]
            piece = piece.reshape(size, ROWS + PAD, LANES)[:, :ROWS]
            out[:size, :, h * LANES : (h + 1) * LANES] = piece.astype(out.dtype)
        row += size
        if s in carry and first == 0:
            window = max(LANES, band)
            begin = partner(me, s, count) * band
            tile = pl.multiple_of(begin // window * window, LANES)
            across = out.shape[2] // band
            for line in range(0, rest[0].shape[0], ROWS):
                place, part = size + line // ROWS // across, line // ROWS % across
                values = rest[0][pl.ds(line, ROWS), pl.ds(tile, window)].astype(jnp.float32)
                own_values = values[:, :band]
                for k in range(band, window, band):
                    own_values = jnp.where(begin - tile == k, values[:, k : k + band], own_values)
                out[place, :, part * band : (part + 1) * band] = own_values.astype(out.dtype)


def rows_for_fields(lines, band, orbitals):
    return -(-lines * band // (ROWS * orbitals))


def apply_y(walkers, kinetic_y, fields, count, cuts, sizes, carry):
    lines, width, orbitals = walkers.shape
    depth = sum(size for _, _, size in cuts)
    used = max(sizes)
    extra = rows_for_fields(lines, width // count, orbitals)

    def out_rows(cut):
        return cut[2] + (extra if cut[0] in carry and cut[1] == 0 else 0)

    def out_spec(cut, size):
        late = (used - size) // ROWS
        return pl.BlockSpec(
            (out_rows(cut), ROWS, orbitals),
            lambda i: (0, jnp.maximum(i - late, 0) if late else i, 0),
        )

    return pl.pallas_call(
        functools.partial(y_kernel, count, width // count, cuts, carry),
        grid=(used // ROWS,),
        in_specs=[
            pl.BlockSpec((ROWS, width, orbitals), lambda i: (i, 0, 0)),
            pl.BlockSpec((width, width), lambda i: (0, 0)),
            pl.BlockSpec((lines, width), lambda i: (0, 0)),
        ],
        out_specs=[out_spec(cut, size) for cut, size in zip(cuts, sizes)],
        out_shape=[
            jax.ShapeDtypeStruct((out_rows(cut), size, orbitals), jnp.bfloat16)
            for cut, size in zip(cuts, sizes)
        ],
        scratch_shapes=[
            pltpu.VMEM((depth, width), jnp.bfloat16),
            pltpu.VMEM((orbitals // LANES, (depth + 1) * (ROWS + PAD), LANES), jnp.float32),
        ],
        **settings(VMEM_MOST),
    )(walkers, kinetic_y, fields)


def x_kernel(count, group, *refs):
    pieces, (field, kinetic, before) = refs[: -count - 4], refs[-count - 4 : -count - 1]
    outs, gram = refs[-count - 1 : -1], refs[-1]

    @pl.when(pl.program_id(0) == 0)
    def _():
        gram[...] = before[...]

    factor = jnp.exp(field[0].astype(jnp.float32))
    total = jnp.zeros(gram.shape, jnp.float32)
    for j in range(group):
        lines = jnp.concatenate([piece[j] for piece in pieces], axis=0)
        moved = jnp.dot(kinetic[...], lines, preferred_element_type=jnp.float32)
        moved = moved.astype(jnp.bfloat16).astype(jnp.float32)
        scaled = (factor[:, j : j + 1] * moved).astype(jnp.bfloat16)
        block = scaled.shape[0] // count
        for t in range(count):
            outs[t][j] = scaled[t * block : (t + 1) * block]
        total += lax.dot_general(
            scaled, scaled, (((0,), (0,)), ((), ())), preferred_element_type=jnp.float32
        )
    gram[...] += total


def apply_x(pieces, fields, kinetic_x, gram, count, first, part):
    orbitals = gram.shape[0]
    length = kinetic_x.shape[0]
    group = fields.shape[2]

    def spec(array, begin):
        offset = (first - begin) // group
        return pl.BlockSpec((group,) + array.shape[1:], lambda i: (i + offset, 0, 0))

    square = pl.BlockSpec((orbitals, orbitals), lambda i: (0, 0))
    out = (part, length // count, orbitals)
    results = pl.pallas_call(
        functools.partial(x_kernel, count, group),
        grid=(part // group,),
        in_specs=[spec(*piece) for piece in pieces]
        + [
            pl.BlockSpec((1, length, group), lambda i: (i + first // group, 0, 0)),
            pl.BlockSpec((length, length), lambda i: (0, 0)),
            square,
        ],
        out_specs=[pl.BlockSpec((group,) + out[1:], lambda i: (i, 0, 0))] * count + [square],
        out_shape=[jax.ShapeDtypeStruct(out, jnp.bfloat16)] * count
        + [jax.ShapeDtypeStruct((orbitals, orbitals), jnp.float32)],
        **settings(),
    )(*[array for array, _ in pieces], fields, kinetic_x, gram)
    return results[:count], results[count]


def times_inverse(piece, inverse, turned, out):
    part, rows, _ = piece.shape
    product = jnp.dot(
        piece[...].reshape(part * rows, piece.shape[2]),
        inverse[...],
        preferred_element_type=jnp.float32,
    )
    for h in range(turned.shape[0]):
        for y in range(part):
            lines = product[y * rows : (y + 1) * rows, h * LANES : (h + 1) * LANES]
            turned[h, pl.ds(y * (rows + PAD), rows), :] = lines
        for r in range(rows):
            line = turned[h, pl.ds(r, part, stride=rows + PAD), :]
            out[r, :, h * LANES : (h + 1) * LANES] = line.astype(out.dtype)


def last_kernel(where, piece, inverse, *rest):
    times_inverse(piece, inverse, rest[-1], rest[-2])


def split_kernel(piece, inverse, *rest):
    for k, out in enumerate(rest[:-1]):
        pl.when(pl.program_id(0) == k)(
            functools.partial(times_inverse, piece, inverse, rest[-1], out)
        )


def place_kernel(where, piece, result, out):
    out[...] = piece[...]


def split(piece, inverse):
    part, lines, orbitals = piece.shape
    rows = 4 * ROWS if lines % (4 * ROWS) == 0 else lines
    out = (rows, part, orbitals)
    return pl.pallas_call(
        split_kernel,
        grid=(lines // rows,),
        in_specs=[
            pl.BlockSpec((part, rows, orbitals), lambda i: (0, i, 0)),
            pl.BlockSpec((orbitals, orbitals), lambda i: (0, 0)),
        ],
        out_specs=[pl.BlockSpec(out, lambda i: (0, 0, 0))] * (lines // rows),
        out_shape=[jax.ShapeDtypeStruct(out, jnp.bfloat16)] * (lines // rows),
        scratch_shapes=[pltpu.VMEM((orbitals // LANES, (part + 1) * (rows + PAD), LANES), jnp.float32)],
        **settings(VMEM_LEAST),
    )(piece, inverse)


def place(result, piece, begin, where):
    lines, part, orbitals = piece.shape
    rows = lines // 2 if begin % (lines // 2) == 0 else lines
    block = (rows, part, orbitals)
    return pl.pallas_call(
        place_kernel,
        grid_spec=pltpu.PrefetchScalarGridSpec(
            num_scalar_prefetch=1,
            grid=(lines // rows,),
            in_specs=[
                pl.BlockSpec(block, lambda i, where: (i, 0, 0)),
                pl.BlockSpec(memory_space=pl.ANY),
            ],
            out_specs=pl.BlockSpec(block, lambda i, where: (begin // rows + i, where[0], 0)),
        ),
        out_shape=jax.ShapeDtypeStruct(result.shape, result.dtype),
        input_output_aliases={2: 0},
        **settings(VMEM_LEAST),
    )(where.reshape(1), piece, result)


def finish(result, piece, inverse, place, width):
    part, lines, orbitals = piece.shape
    begun = result is not None
    rows = 4 * ROWS if lines % (4 * ROWS) == 0 else ROWS
    return pl.pallas_call(
        last_kernel,
        grid_spec=pltpu.PrefetchScalarGridSpec(
            num_scalar_prefetch=1,
            grid=(lines // rows,),
            in_specs=[
                pl.BlockSpec((part, rows, orbitals), lambda i, where: (0, i, 0)),
                pl.BlockSpec((orbitals, orbitals), lambda i, where: (0, 0)),
            ]
            + [pl.BlockSpec(memory_space=pl.ANY)] * begun,
            out_specs=pl.BlockSpec((rows, part, orbitals), lambda i, where: (i, where[0], 0)),
            scratch_shapes=[pltpu.VMEM((orbitals // LANES, (part + 1) * (rows + PAD), LANES), jnp.float32)],
        ),
        out_shape=jax.ShapeDtypeStruct((lines, width, orbitals), jnp.bfloat16),
        input_output_aliases={3: 0} if begun else {},
        **settings(VMEM_LEAST),
    )(place.reshape(1), piece, inverse, *([result] if begun else []))


def factor_kernel(scale, first, second, lower, inverse, work, upper):
    size = lower.shape[0]
    quarter = size // 4
    upper[3 * quarter :, :] = first[:, :size]
    upper[:quarter, :quarter] = first[:, size:]
    upper[2 * quarter : 3 * quarter, : 3 * quarter] = second[:, : 3 * quarter]
    upper[quarter : 2 * quarter, : 2 * quarter] = second[:, 3 * quarter :]
    row = lax.broadcasted_iota(jnp.int32, (size, size), 0)
    column = lax.broadcasted_iota(jnp.int32, (size, size), 1)
    work[:, :size] = jnp.where(row >= column, upper[...], upper[...].T) * scale
    work[:, size:] = jnp.where(row == column, 1.0, 0.0)
    line = lax.broadcasted_iota(jnp.int32, (BLOCK, 2 * BLOCK), 0)
    lane = lax.broadcasted_iota(jnp.int32, (BLOCK, 2 * BLOCK), 1)
    identity = jnp.where(lane == line, 1.0, 0.0)[:, :BLOCK]
    dot = functools.partial(
        jnp.dot, precision=lax.Precision.HIGHEST, preferred_element_type=jnp.float32
    )
    for begin in range(0, size, BLOCK):
        end = begin + BLOCK
        both = jnp.concatenate([work[begin:end, begin:end], identity], axis=1)
        for j in range(BLOCK):
            pivot_column = jnp.broadcast_to(both[:, j : j + 1], both.shape)
            pivot = jnp.broadcast_to(pivot_column[j : j + 1], both.shape)
            root = lax.rsqrt(pivot)
            root = root * (1.5 - 0.5 * pivot * root * root)
            pivot_row = jnp.broadcast_to(both[j : j + 1], both.shape) * root
            below = both - pivot_column * root * pivot_row
            both = jnp.where(line > j, below, jnp.where(line == j, pivot_row, both))
        panel = dot(both[:, BLOCK:], work[begin:end, :])
        upper[begin:end, :] = panel[:, :size]
        work[begin:end, size:] = panel[:, size:]
        if end < size:
            work[end:, :] -= dot(panel[:, end:size].T, panel)
    lower[...] = jnp.where(row >= column, upper[...].T, 0.0)
    inverse[...] = work[:, size:].T.astype(inverse.dtype)


def pack(gram):
    quarter = gram.shape[0] // 4
    first = [gram[3 * quarter :], gram[:quarter, :quarter]]
    second = [gram[2 * quarter : 3 * quarter, : 3 * quarter], gram[quarter : 2 * quarter, : 2 * quarter]]
    return jnp.concatenate(first, axis=1), jnp.concatenate(second, axis=1)


def factor(first, second, scale):
    size = first.shape[0] * 4
    return pl.pallas_call(
        functools.partial(factor_kernel, scale),
        out_shape=[
            jax.ShapeDtypeStruct((size, size), jnp.float32),
            jax.ShapeDtypeStruct((size, size), jnp.bfloat16),
        ],
        scratch_shapes=[
            pltpu.VMEM((size, 2 * size), jnp.float32),
            pltpu.VMEM((size, size), jnp.float32),
        ],
        **settings(VMEM_LEAST),
    )(first, second)


def one_determinant(walkers, fields, kinetic_x, kinetic_y, count):
    lines, width, orbitals = walkers.shape
    me = lax.axis_index("site")
    band = width // count
    part = ROWS if band % ROWS == 0 else band
    chunks = band // part
    group = 8 if part % 8 == 0 else part
    wide = 2 * part if band % (2 * part) == 0 else band
    steps = range(count)
    order = jnp.stack([partner(me, s, count) for s in steps])

    extra = rows_for_fields(lines, band, orbitals)
    far = [s for s in steps if s > 1 and lines > ROWS]
    near = [s for s in steps if s not in far]
    head = {}
    if far:
        cuts = [(s, 0, band) for s in far]
        arrays = apply_y(walkers, kinetic_y, fields, count, cuts, [ROWS] * len(far), far)
        kinetic_y, *arrays = tie(kinetic_y, *arrays)
        head = {s: trade(a, s, count) for s, a in zip(far, arrays)}
    near_cuts = [(0, part), (part, part), (2 * part, band - 2 * part)] if chunks >= 4 else [(0, band)]
    cuts = [(s, first, wide) for first in range(0, band, wide) for s in far]
    cuts += [(s, *cut) for s in near for cut in ([(0, band)] if s == 0 or not far else near_cuts)]
    sizes = [lines if s in near else lines - ROWS for s, _, _ in cuts]
    arrays = apply_y(walkers, kinetic_y, fields, count, cuts, sizes, near)
    tail = {(s, first): a for (s, first, _), a in zip(cuts, arrays)}
    def hold(key, *keys):
        held = tie(tail[key], *[tail[k] if isinstance(k, tuple) else head[k] for k in keys])
        tail[key] = held[0]
        for k, array in zip(keys, held[1:]):
            (tail if isinstance(k, tuple) else head)[k] = array

    sent = set()

    def go(key):
        tail[key] = trade(tail[key], key[0], count)
        sent.add(key)

    for s in far:
        go((s, 0))
    if far and chunks >= 4:
        y, z = (near[-1], 0), (near[-1], part)
        hold(y, *far)
        go(y)
        hold(z, y, *[(s, 0) for s in far])
        go(z)
    for key in tail:
        if key not in sent:
            go(key)
    own_fields = []
    for s in steps:
        sent = (head[s] if s in far else tail[s, 0])[-extra:, :ROWS]
        sent = sent.reshape(extra, ROWS, orbitals // band, band)
        own_fields.append(jnp.swapaxes(sent, 1, 2).reshape(-1, band)[:lines])
    own_fields = jnp.stack(own_fields)
    own_fields = own_fields.reshape(count * lines, band // group, group).swapaxes(0, 1)
    turned_x = kinetic_x.reshape(count, lines, count, lines)
    turned_x = jnp.take(jnp.take(turned_x, order, axis=0), order, axis=2).reshape(kinetic_x.shape)

    gram = jnp.zeros((orbitals, orbitals), jnp.float32)
    ready = []
    for first in range(0, band, part):
        pieces = []
        for s in steps:
            if s in far:
                pieces.append((head[s], 0))
            begin = max(at for step, at in tail if step == s and at <= first)
            pieces.append((tail[s, begin], begin))
        scaled, gram = apply_x(pieces, own_fields, turned_x, gram, count, first, part)
        ready.append(scaled)

    back = []
    for c in range(min(2, len(ready))):
        back.append(dict(enumerate(ready[c])))
        for s in far:
            if c == 1 and (s, wide) in tail:
                back[c][s], tail[s, wide] = tie(back[c][s], tail[s, wide])
            if c == 1 and s != far[0]:
                back[c][s], back[0][far[-1]] = tie(back[c][s], back[0][far[-1]])
            back[c][s] = trade(back[c][s], s, count)
    if count & (count - 1) == 0 and count > 1:
        core = me & 1
        if far:
            gram, back[0][far[0]] = tie(gram, back[0][far[0]])
        first, second = pack(gram)
        mine = jnp.where(core == 0, first, second)
        mine = mine + trade(jnp.where(core == 0, second, first), 1, count)
        step = 2
        while step < count:
            mine = mine + trade(mine, step, count)
            step *= 2
        if len(back) > 1 and far:
            mine, back[1][far[0]] = tie(mine, back[1][far[0]])
        other = trade(mine, 1, count)
        first, second = jnp.where(core == 0, mine, other), jnp.where(core == 0, other, mine)
    else:
        first, second = pack(lax.psum(gram, "site"))
    lower, inverse = factor(first, second, 1.0 / (count * lines * width))

    for c in range(2, len(ready)):
        back.append(dict(enumerate(ready[c])))
        for s in far:
            if c == 2:
                back[c][s], back[0][s] = tie(back[c][s], back[0][s])
            elif c < chunks - 1:
                back[c][s], inverse = tie(back[c][s], inverse)
            if 2 < c == chunks - 1:
                back[c][s] = [trade(piece, s, count) for piece in split(back[c][s], inverse)]
            else:
                back[c][s] = trade(back[c][s], s, count)
    for c in range(len(back)):
        for s in near:
            back[c][s], first = tie(back[c][s], first)
            back[c][s] = trade(back[c][s], s, count)

    result = None
    for c in range(chunks):
        for s in steps:
            if not isinstance(back[c][s], list):
                where = order[s] * chunks + c
                result = finish(result, back[c][s], inverse, where, width)
    for s in far:
        if isinstance(back[-1][s], list):
            pieces = back[-1][s]
            for k, piece in enumerate(pieces):
                where = order[s] * chunks + chunks - 1
                result = place(result, piece, k * piece.shape[0], where)
    return result, lower


def per_device(count, walkers, fields, kinetic_x, kinetic_y):
    results = [
        one_determinant(walkers[i], fields[i, 0], kinetic_x, kinetic_y, count)
        for i in range(walkers.shape[0])
    ]
    return tuple(jnp.stack(part) for part in zip(*results))


def solution(mesh):
    placed = (
        P(("grp", "spin"), "site", None, None),
        P(("grp", "spin"), None, "site", None),
        P(),
        P(),
    )
    return jax.shard_map(
        functools.partial(per_device, mesh.shape["site"]),
        mesh=mesh,
        in_specs=placed,
        out_specs=(P(("grp", "spin"), "site", None, None), P(("grp", "spin"), None, None)),
        check_vma=False,
    )
```

```python
import functools

import jax
import jax.numpy as jnp
from jax import lax
from jax.experimental import pallas as pl
from jax.experimental.pallas import tpu as pltpu
from jax.sharding import PartitionSpec as P

ROWS = 16
LANES = 128
PAD = 8
PARTS = 2
BLOCK = 64
VMEM_LIMIT = 20 * 1024 * 1024
VMEM_LEAST = 8 * 1024 * 1024
VMEM_MOST = 56 * 1024 * 1024


def partner(device, step, count):
    if count & (count - 1) == 0:
        return device ^ step
    return (step - device + count) % count


def trade(piece, step, count):
    if step == 0 and count & (count - 1) == 0:
        return piece
    return lax.ppermute(piece, "site", [(i, partner(i, step, count)) for i in range(count)])


def tie(*arrays):
    return lax.optimization_barrier(arrays)


def settings(limit=VMEM_LIMIT):
    return dict(
        compiler_params=pltpu.CompilerParams(vmem_limit_bytes=limit),
        cost_estimate=pl.CostEstimate(flops=1000, bytes_accessed=1000, transcendentals=0),
    )


def y_kernel(count, band, cuts, carry, walkers, kinetic, *rest):
    outs, own, turned = rest[-2 - len(cuts) : -2], rest[-2], rest[-1]
    me = lax.axis_index("site")
    depth = own.shape[0]

    @pl.when(pl.program_id(0) == 0)
    def _():
        row = 0
        for s, first, size in cuts:
            start = pl.multiple_of(partner(me, s, count) * band + first, ROWS)
            own[pl.ds(row, size), :] = kinetic[pl.ds(start, size), :]
            row += size

    for r in range(ROWS):
        line = jnp.dot(own[...], walkers[r], preferred_element_type=jnp.float32)
        for h in range(turned.shape[0]):
            part = line[:, h * LANES : (h + 1) * LANES]
            turned[h, pl.ds(r, depth, stride=ROWS + PAD), :] = part
    row = 0
    for (s, first, size), out in zip(cuts, outs):
        for h in range(turned.shape[0]):
            piece = turned[h, pl.ds(row * (ROWS + PAD), size * (ROWS + PAD)), :]
            piece = piece.reshape(size, ROWS + PAD, LANES)[:, :ROWS]
            out[:size, :, h * LANES : (h + 1) * LANES] = piece.astype(out.dtype)
        row += size
        if s in carry and first == 0:
            window = max(LANES, band)
            begin = partner(me, s, count) * band
            tile = pl.multiple_of(begin // window * window, LANES)
            across = out.shape[2] // band
            for line in range(0, rest[0].shape[0], ROWS):
                place, part = size + line // ROWS // across, line // ROWS % across
                values = rest[0][pl.ds(line, ROWS), pl.ds(tile, window)].astype(jnp.float32)
                own_values = values[:, :band]
                for k in range(band, window, band):
                    own_values = jnp.where(begin - tile == k, values[:, k : k + band], own_values)
                out[place, :, part * band : (part + 1) * band] = own_values.astype(out.dtype)


def rows_for_fields(lines, band, orbitals):
    return -(-lines * band // (ROWS * orbitals))


def apply_y(walkers, kinetic_y, fields, count, cuts, sizes, carry):
    lines, width, orbitals = walkers.shape
    depth = sum(size for _, _, size in cuts)
    used = max(sizes)
    extra = rows_for_fields(lines, width // count, orbitals)

    def out_rows(cut):
        return cut[2] + (extra if cut[0] in carry and cut[1] == 0 else 0)

    def out_spec(cut, size):
        late = (used - size) // ROWS
        return pl.BlockSpec(
            (out_rows(cut), ROWS, orbitals),
            lambda i: (0, jnp.maximum(i - late, 0) if late else i, 0),
        )

    return pl.pallas_call(
        functools.partial(y_kernel, count, width // count, cuts, carry),
        grid=(used // ROWS,),
        in_specs=[
            pl.BlockSpec((ROWS, width, orbitals), lambda i: (i, 0, 0)),
            pl.BlockSpec((width, width), lambda i: (0, 0)),
            pl.BlockSpec((lines, width), lambda i: (0, 0)),
        ],
        out_specs=[out_spec(cut, size) for cut, size in zip(cuts, sizes)],
        out_shape=[
            jax.ShapeDtypeStruct((out_rows(cut), size, orbitals), jnp.bfloat16)
            for cut, size in zip(cuts, sizes)
        ],
        scratch_shapes=[
            pltpu.VMEM((depth, width), jnp.bfloat16),
            pltpu.VMEM((orbitals // LANES, (depth + 1) * (ROWS + PAD), LANES), jnp.float32),
        ],
        **settings(VMEM_MOST),
    )(walkers, kinetic_y, fields)


def x_kernel(count, group, *refs):
    pieces, (field, kinetic, before) = refs[: -count - 4], refs[-count - 4 : -count - 1]
    outs, gram = refs[-count - 1 : -1], refs[-1]

    @pl.when(pl.program_id(0) == 0)
    def _():
        gram[...] = before[...]

    factor = jnp.exp(field[0].astype(jnp.float32))
    total = jnp.zeros(gram.shape, jnp.float32)
    for j in range(group):
        lines = jnp.concatenate([piece[j] for piece in pieces], axis=0)
        moved = jnp.dot(kinetic[...], lines, preferred_element_type=jnp.float32)
        moved = moved.astype(jnp.bfloat16).astype(jnp.float32)
        scaled = (factor[:, j : j + 1] * moved).astype(jnp.bfloat16)
        block = scaled.shape[0] // count
        for t in range(count):
            outs[t][j] = scaled[t * block : (t + 1) * block]
        total += lax.dot_general(
            scaled, scaled, (((0,), (0,)), ((), ())), preferred_element_type=jnp.float32
        )
    gram[...] += total


def apply_x(pieces, fields, kinetic_x, gram, count, first, part):
    orbitals = gram.shape[0]
    length = kinetic_x.shape[0]
    group = fields.shape[2]

    def spec(array, begin):
        offset = (first - begin) // group
        return pl.BlockSpec((group,) + array.shape[1:], lambda i: (i + offset, 0, 0))

    square = pl.BlockSpec((orbitals, orbitals), lambda i: (0, 0))
    out = (part, length // count, orbitals)
    results = pl.pallas_call(
        functools.partial(x_kernel, count, group),
        grid=(part // group,),
        in_specs=[spec(*piece) for piece in pieces]
        + [
            pl.BlockSpec((1, length, group), lambda i: (i + first // group, 0, 0)),
            pl.BlockSpec((length, length), lambda i: (0, 0)),
            square,
        ],
        out_specs=[pl.BlockSpec((group,) + out[1:], lambda i: (i, 0, 0))] * count + [square],
        out_shape=[jax.ShapeDtypeStruct(out, jnp.bfloat16)] * count
        + [jax.ShapeDtypeStruct((orbitals, orbitals), jnp.float32)],
        **settings(),
    )(*[array for array, _ in pieces], fields, kinetic_x, gram)
    return results[:count], results[count]


def times_inverse(piece, inverse, turned, out):
    part, rows, _ = piece.shape
    product = jnp.dot(
        piece[...].reshape(part * rows, piece.shape[2]),
        inverse[...],
        preferred_element_type=jnp.float32,
    )
    for h in range(turned.shape[0]):
        for y in range(part):
            lines = product[y * rows : (y + 1) * rows, h * LANES : (h + 1) * LANES]
            turned[h, pl.ds(y * (rows + PAD), rows), :] = lines
        for r in range(rows):
            line = turned[h, pl.ds(r, part, stride=rows + PAD), :]
            out[r, :, h * LANES : (h + 1) * LANES] = line.astype(out.dtype)


def last_kernel(where, piece, inverse, *rest):
    times_inverse(piece, inverse, rest[-1], rest[-2])


def split_kernel(piece, inverse, *rest):
    for k, out in enumerate(rest[:-1]):
        pl.when(pl.program_id(0) == k)(
            functools.partial(times_inverse, piece, inverse, rest[-1], out)
        )


def place_kernel(begin, step, count, chunk, chunks, piece, result, out, held, got, put):
    lines, part, _ = piece.shape
    rows = lines // got.shape[0]
    where = partner(lax.axis_index("site"), step, count) * chunks + chunk
    y = pl.ds(pl.multiple_of(where * part, ROWS), part)
    reads, writes = [], []
    for k in range(got.shape[0]):
        x = pl.ds(k * rows, rows)
        reads.append(pltpu.make_async_copy(piece.at[x], held.at[x], got.at[k]))
        target = out.at[pl.ds(begin + k * rows, rows), y, :]
        writes.append(pltpu.make_async_copy(held.at[x], target, put.at[k]))
    for read in reads:
        read.start()
    for read, write in zip(reads, writes):
        read.wait()
        write.start()
    for write in writes:
        write.wait()


def split(piece, inverse):
    part, lines, orbitals = piece.shape
    rows = 4 * ROWS if lines % (4 * ROWS) == 0 else lines
    out = (rows, part, orbitals)
    return pl.pallas_call(
        split_kernel,
        grid=(lines // rows,),
        in_specs=[
            pl.BlockSpec((part, rows, orbitals), lambda i: (0, i, 0)),
            pl.BlockSpec((orbitals, orbitals), lambda i: (0, 0)),
        ],
        out_specs=[pl.BlockSpec(out, lambda i: (0, 0, 0))] * (lines // rows),
        out_shape=[jax.ShapeDtypeStruct(out, jnp.bfloat16)] * (lines // rows),
        scratch_shapes=[pltpu.VMEM((orbitals // LANES, (part + 1) * (rows + PAD), LANES), jnp.float32)],
        **settings(VMEM_LEAST),
    )(piece, inverse)


def place(result, piece, begin, step, count, chunk, chunks):
    parts = PARTS if piece.shape[0] % PARTS == 0 else 1
    anywhere = pl.BlockSpec(memory_space=pl.ANY)
    return pl.pallas_call(
        functools.partial(place_kernel, begin, step, count, chunk, chunks),
        in_specs=[anywhere, anywhere],
        out_specs=anywhere,
        out_shape=jax.ShapeDtypeStruct(result.shape, result.dtype),
        scratch_shapes=[
            pltpu.VMEM(piece.shape, jnp.bfloat16),
            pltpu.SemaphoreType.DMA((parts,)),
            pltpu.SemaphoreType.DMA((parts,)),
        ],
        input_output_aliases={1: 0},
        **settings(VMEM_LEAST),
    )(piece, result)


def finish(result, piece, inverse, place, width):
    part, lines, orbitals = piece.shape
    begun = result is not None
    rows = 4 * ROWS if lines % (4 * ROWS) == 0 else ROWS
    return pl.pallas_call(
        last_kernel,
        grid_spec=pltpu.PrefetchScalarGridSpec(
            num_scalar_prefetch=1,
            grid=(lines // rows,),
            in_specs=[
                pl.BlockSpec((part, rows, orbitals), lambda i, where: (0, i, 0)),
                pl.BlockSpec((orbitals, orbitals), lambda i, where: (0, 0)),
            ]
            + [pl.BlockSpec(memory_space=pl.ANY)] * begun,
            out_specs=pl.BlockSpec((rows, part, orbitals), lambda i, where: (i, where[0], 0)),
            scratch_shapes=[pltpu.VMEM((orbitals // LANES, (part + 1) * (rows + PAD), LANES), jnp.float32)],
        ),
        out_shape=jax.ShapeDtypeStruct((lines, width, orbitals), jnp.bfloat16),
        input_output_aliases={3: 0} if begun else {},
        **settings(VMEM_LEAST),
    )(place.reshape(1), piece, inverse, *([result] if begun else []))


def factor_kernel(scale, first, second, lower, inverse, work, upper):
    size = lower.shape[0]
    quarter = size // 4
    upper[3 * quarter :, :] = first[:, :size]
    upper[:quarter, :quarter] = first[:, size:]
    upper[2 * quarter : 3 * quarter, : 3 * quarter] = second[:, : 3 * quarter]
    upper[quarter : 2 * quarter, : 2 * quarter] = second[:, 3 * quarter :]
    row = lax.broadcasted_iota(jnp.int32, (size, size), 0)
    column = lax.broadcasted_iota(jnp.int32, (size, size), 1)
    work[:, :size] = jnp.where(row >= column, upper[...], upper[...].T) * scale
    work[:, size:] = jnp.where(row == column, 1.0, 0.0)
    line = lax.broadcasted_iota(jnp.int32, (BLOCK, 2 * BLOCK), 0)
    lane = lax.broadcasted_iota(jnp.int32, (BLOCK, 2 * BLOCK), 1)
    identity = jnp.where(lane == line, 1.0, 0.0)[:, :BLOCK]
    dot = functools.partial(
        jnp.dot, precision=lax.Precision.HIGHEST, preferred_element_type=jnp.float32
    )
    for begin in range(0, size, BLOCK):
        end = begin + BLOCK
        both = jnp.concatenate([work[begin:end, begin:end], identity], axis=1)
        for j in range(BLOCK):
            pivot_column = jnp.broadcast_to(both[:, j : j + 1], both.shape)
            pivot = jnp.broadcast_to(pivot_column[j : j + 1], both.shape)
            root = lax.rsqrt(pivot)
            root = root * (1.5 - 0.5 * pivot * root * root)
            pivot_row = jnp.broadcast_to(both[j : j + 1], both.shape) * root
            below = both - pivot_column * root * pivot_row
            both = jnp.where(line > j, below, jnp.where(line == j, pivot_row, both))
        panel = dot(both[:, BLOCK:], work[begin:end, :])
        upper[begin:end, :] = panel[:, :size]
        work[begin:end, size:] = panel[:, size:]
        if end < size:
            work[end:, :] -= dot(panel[:, end:size].T, panel)
    lower[...] = jnp.where(row >= column, upper[...].T, 0.0)
    inverse[...] = work[:, size:].T.astype(inverse.dtype)


def pack(gram):
    quarter = gram.shape[0] // 4
    first = [gram[3 * quarter :], gram[:quarter, :quarter]]
    second = [gram[2 * quarter : 3 * quarter, : 3 * quarter], gram[quarter : 2 * quarter, : 2 * quarter]]
    return jnp.concatenate(first, axis=1), jnp.concatenate(second, axis=1)


def factor(first, second, scale):
    size = first.shape[0] * 4
    return pl.pallas_call(
        functools.partial(factor_kernel, scale),
        out_shape=[
            jax.ShapeDtypeStruct((size, size), jnp.float32),
            jax.ShapeDtypeStruct((size, size), jnp.bfloat16),
        ],
        scratch_shapes=[
            pltpu.VMEM((size, 2 * size), jnp.float32),
            pltpu.VMEM((size, size), jnp.float32),
        ],
        **settings(VMEM_LEAST),
    )(first, second)


def one_determinant(walkers, fields, kinetic_x, kinetic_y, count):
    lines, width, orbitals = walkers.shape
    me = lax.axis_index("site")
    band = width // count
    part = ROWS if band % ROWS == 0 else band
    chunks = band // part
    group = 8 if part % 8 == 0 else part
    wide = 2 * part if band % (2 * part) == 0 else band
    steps = range(count)
    order = jnp.stack([partner(me, s, count) for s in steps])

    extra = rows_for_fields(lines, band, orbitals)
    far = [s for s in steps if s > 1 and lines > ROWS]
    near = [s for s in steps if s not in far]
    head = {}
    if far:
        cuts = [(s, 0, band) for s in far]
        arrays = apply_y(walkers, kinetic_y, fields, count, cuts, [ROWS] * len(far), far)
        kinetic_y, *arrays = tie(kinetic_y, *arrays)
        head = {s: trade(a, s, count) for s, a in zip(far, arrays)}
    near_cuts = [(0, part), (part, part), (2 * part, band - 2 * part)] if chunks >= 4 else [(0, band)]
    cuts = [(s, first, wide) for first in range(0, band, wide) for s in far]
    cuts += [(s, *cut) for s in near for cut in ([(0, band)] if s == 0 or not far else near_cuts)]
    sizes = [lines if s in near else lines - ROWS for s, _, _ in cuts]
    arrays = apply_y(walkers, kinetic_y, fields, count, cuts, sizes, near)
    tail = {(s, first): a for (s, first, _), a in zip(cuts, arrays)}
    def hold(key, *keys):
        held = tie(tail[key], *[tail[k] if isinstance(k, tuple) else head[k] for k in keys])
        tail[key] = held[0]
        for k, array in zip(keys, held[1:]):
            (tail if isinstance(k, tuple) else head)[k] = array

    sent = set()

    def go(key):
        tail[key] = trade(tail[key], key[0], count)
        sent.add(key)

    for s in far:
        go((s, 0))
    if far and chunks >= 4:
        y, z = (near[-1], 0), (near[-1], part)
        hold(y, *far)
        go(y)
        hold(z, y, *[(s, 0) for s in far])
        go(z)
    for key in tail:
        if key not in sent:
            go(key)
    own_fields = []
    for s in steps:
        sent = (head[s] if s in far else tail[s, 0])[-extra:, :ROWS]
        sent = sent.reshape(extra, ROWS, orbitals // band, band)
        own_fields.append(jnp.swapaxes(sent, 1, 2).reshape(-1, band)[:lines])
    own_fields = jnp.stack(own_fields)
    own_fields = own_fields.reshape(count * lines, band // group, group).swapaxes(0, 1)
    turned_x = kinetic_x.reshape(count, lines, count, lines)
    turned_x = jnp.take(jnp.take(turned_x, order, axis=0), order, axis=2).reshape(kinetic_x.shape)

    gram = jnp.zeros((orbitals, orbitals), jnp.float32)
    ready = []
    for first in range(0, band, part):
        pieces = []
        for s in steps:
            if s in far:
                pieces.append((head[s], 0))
            begin = max(at for step, at in tail if step == s and at <= first)
            pieces.append((tail[s, begin], begin))
        scaled, gram = apply_x(pieces, own_fields, turned_x, gram, count, first, part)
        ready.append(scaled)

    back = []
    for c in range(min(2, len(ready))):
        back.append(dict(enumerate(ready[c])))
        for s in far:
            if c == 1 and (s, wide) in tail:
                back[c][s], tail[s, wide] = tie(back[c][s], tail[s, wide])
            if c == 1 and s != far[0]:
                back[c][s], back[0][far[-1]] = tie(back[c][s], back[0][far[-1]])
            back[c][s] = trade(back[c][s], s, count)
    if count & (count - 1) == 0 and count > 1:
        core = me & 1
        if far:
            gram, back[0][far[0]] = tie(gram, back[0][far[0]])
        first, second = pack(gram)
        mine = jnp.where(core == 0, first, second)
        mine = mine + trade(jnp.where(core == 0, second, first), 1, count)
        step = 2
        while step < count:
            mine = mine + trade(mine, step, count)
            step *= 2
        if len(back) > 1 and far:
            mine, back[1][far[0]] = tie(mine, back[1][far[0]])
        other = trade(mine, 1, count)
        first, second = jnp.where(core == 0, mine, other), jnp.where(core == 0, other, mine)
    else:
        first, second = pack(lax.psum(gram, "site"))
    lower, inverse = factor(first, second, 1.0 / (count * lines * width))

    for c in range(2, len(ready)):
        back.append(dict(enumerate(ready[c])))
        for s in far:
            if c == 2:
                back[c][s], back[0][s] = tie(back[c][s], back[0][s])
            elif c < chunks - 1:
                back[c][s], inverse = tie(back[c][s], inverse)
            if 2 < c == chunks - 1:
                back[c][s] = [trade(piece, s, count) for piece in split(back[c][s], inverse)]
            else:
                back[c][s] = trade(back[c][s], s, count)
    for c in range(len(back)):
        for s in near:
            back[c][s], first = tie(back[c][s], first)
            back[c][s] = trade(back[c][s], s, count)

    result = None
    for c in range(chunks):
        for s in steps:
            if not isinstance(back[c][s], list):
                where = order[s] * chunks + c
                result = finish(result, back[c][s], inverse, where, width)
    for s in far:
        if isinstance(back[-1][s], list):
            pieces = back[-1][s]
            for k, piece in enumerate(pieces):
                at = k * piece.shape[0]
                result = place(result, piece, at, s, count, chunks - 1, chunks)
    return result, lower


def per_device(count, walkers, fields, kinetic_x, kinetic_y):
    results = [
        one_determinant(walkers[i], fields[i, 0], kinetic_x, kinetic_y, count)
        for i in range(walkers.shape[0])
    ]
    return tuple(jnp.stack(part) for part in zip(*results))


def solution(mesh):
    placed = (
        P(("grp", "spin"), "site", None, None),
        P(("grp", "spin"), None, "site", None),
        P(),
        P(),
    )
    return jax.shard_map(
        functools.partial(per_device, mesh.shape["site"]),
        mesh=mesh,
        in_specs=placed,
        out_specs=(P(("grp", "spin"), "site", None, None), P(("grp", "spin"), None, None)),
        check_vma=False,
    )
```

```python
import functools

import jax
import jax.numpy as jnp
from jax import lax
from jax.experimental import pallas as pl
from jax.experimental.pallas import tpu as pltpu
from jax.sharding import PartitionSpec as P

ROWS = 16
LANES = 128
PAD = 8
STEP = 8
BLOCK = 64
VMEM_LIMIT = 20 * 1024 * 1024
VMEM_LEAST = 8 * 1024 * 1024
VMEM_MOST = 56 * 1024 * 1024


def partner(device, step, count):
    if count & (count - 1) == 0:
        return device ^ step
    return (step - device + count) % count


def trade(piece, step, count):
    if step == 0 and count & (count - 1) == 0:
        return piece
    return lax.ppermute(piece, "site", [(i, partner(i, step, count)) for i in range(count)])


def tie(*arrays):
    return lax.optimization_barrier(arrays)


def settings(limit=VMEM_LIMIT):
    return dict(
        compiler_params=pltpu.CompilerParams(vmem_limit_bytes=limit),
        cost_estimate=pl.CostEstimate(flops=1000, bytes_accessed=1000, transcendentals=0),
    )


def y_kernel(count, band, cuts, carry, walkers, kinetic, fields, *rest):
    outs, own, turned = rest[: len(cuts)], rest[len(cuts)], rest[len(cuts) + 1]
    me = lax.axis_index("site")
    depth = own.shape[0]
    copies = []
    if len(rest) > len(cuts) + 2:
        lines, matrix, values, sems = rest[len(cuts) + 2 :]
        pairs = [(kinetic, matrix), (fields, values)]
        for r in range(0, ROWS, STEP):
            pairs.append((walkers.at[pl.ds(r, STEP)], lines.at[pl.ds(r, STEP)]))
        copies = [pltpu.make_async_copy(*pair, sems.at[k]) for k, pair in enumerate(pairs)]
        for copy in copies:
            copy.start()
        copies[0].wait()
        walkers, kinetic, fields = lines, matrix, values

    @pl.when(pl.program_id(0) == 0)
    def _():
        row = 0
        for s, first, size in cuts:
            start = pl.multiple_of(partner(me, s, count) * band + first, ROWS)
            own[pl.ds(row, size), :] = kinetic[pl.ds(start, size), :]
            row += size

    for r in range(ROWS):
        if copies and r % STEP == 0:
            copies[2 + r // STEP].wait()
        line = jnp.dot(own[...], walkers[r], preferred_element_type=jnp.float32)
        for h in range(turned.shape[0]):
            part = line[:, h * LANES : (h + 1) * LANES]
            turned[h, pl.ds(r, depth, stride=ROWS + PAD), :] = part
    if copies:
        copies[1].wait()
    row = 0
    for (s, first, size), out in zip(cuts, outs):
        for h in range(turned.shape[0]):
            piece = turned[h, pl.ds(row * (ROWS + PAD), size * (ROWS + PAD)), :]
            piece = piece.reshape(size, ROWS + PAD, LANES)[:, :ROWS]
            out[:size, :, h * LANES : (h + 1) * LANES] = piece.astype(out.dtype)
        row += size
        if s in carry and first == 0:
            window = max(LANES, band)
            begin = partner(me, s, count) * band
            tile = pl.multiple_of(begin // window * window, LANES)
            across = out.shape[2] // band
            for line in range(0, fields.shape[0], ROWS):
                place, part = size + line // ROWS // across, line // ROWS % across
                values = fields[pl.ds(line, ROWS), pl.ds(tile, window)].astype(jnp.float32)
                own_values = values[:, :band]
                for k in range(band, window, band):
                    own_values = jnp.where(begin - tile == k, values[:, k : k + band], own_values)
                out[place, :, part * band : (part + 1) * band] = own_values.astype(out.dtype)


def rows_for_fields(lines, band, orbitals):
    return -(-lines * band // (ROWS * orbitals))


def apply_y(walkers, kinetic_y, fields, count, cuts, sizes, carry):
    lines, width, orbitals = walkers.shape
    depth = sum(size for _, _, size in cuts)
    used = max(sizes)
    extra = rows_for_fields(lines, width // count, orbitals)

    def out_rows(cut):
        return cut[2] + (extra if cut[0] in carry and cut[1] == 0 else 0)

    def out_spec(cut, size):
        late = (used - size) // ROWS
        return pl.BlockSpec(
            (out_rows(cut), ROWS, orbitals),
            lambda i: (0, jnp.maximum(i - late, 0) if late else i, 0),
        )

    return pl.pallas_call(
        functools.partial(y_kernel, count, width // count, cuts, carry),
        grid=(used // ROWS,),
        in_specs=[pl.BlockSpec(memory_space=pl.ANY)] * 3
        if used == ROWS
        else [
            pl.BlockSpec((ROWS, width, orbitals), lambda i: (i, 0, 0)),
            pl.BlockSpec((width, width), lambda i: (0, 0)),
            pl.BlockSpec((lines, width), lambda i: (0, 0)),
        ],
        out_specs=[out_spec(cut, size) for cut, size in zip(cuts, sizes)],
        out_shape=[
            jax.ShapeDtypeStruct((out_rows(cut), size, orbitals), jnp.bfloat16)
            for cut, size in zip(cuts, sizes)
        ],
        scratch_shapes=[
            pltpu.VMEM((depth, width), jnp.bfloat16),
            pltpu.VMEM((orbitals // LANES, (depth + 1) * (ROWS + PAD), LANES), jnp.float32),
        ]
        + (
            [
                pltpu.VMEM((ROWS, width, orbitals), jnp.bfloat16),
                pltpu.VMEM((width, width), jnp.bfloat16),
                pltpu.VMEM((lines, width), jnp.bfloat16),
                pltpu.SemaphoreType.DMA((2 + ROWS // STEP,)),
            ]
            if used == ROWS
            else []
        ),
        **settings(VMEM_MOST),
    )(walkers, kinetic_y, fields)


def x_kernel(count, group, *refs):
    pieces, (field, kinetic, before) = refs[: -count - 4], refs[-count - 4 : -count - 1]
    outs, gram = refs[-count - 1 : -1], refs[-1]

    @pl.when(pl.program_id(0) == 0)
    def _():
        gram[...] = before[...]

    factor = jnp.exp(field[0].astype(jnp.float32))
    total = jnp.zeros(gram.shape, jnp.float32)
    for j in range(group):
        lines = jnp.concatenate([piece[j] for piece in pieces], axis=0)
        moved = jnp.dot(kinetic[...], lines, preferred_element_type=jnp.float32)
        moved = moved.astype(jnp.bfloat16).astype(jnp.float32)
        scaled = (factor[:, j : j + 1] * moved).astype(jnp.bfloat16)
        block = scaled.shape[0] // count
        for t in range(count):
            outs[t][j] = scaled[t * block : (t + 1) * block]
        total += lax.dot_general(
            scaled, scaled, (((0,), (0,)), ((), ())), preferred_element_type=jnp.float32
        )
    gram[...] += total


def apply_x(pieces, fields, kinetic_x, gram, count, first, part):
    orbitals = gram.shape[0]
    length = kinetic_x.shape[0]
    group = fields.shape[2]

    def spec(array, begin):
        offset = (first - begin) // group
        return pl.BlockSpec((group,) + array.shape[1:], lambda i: (i + offset, 0, 0))

    square = pl.BlockSpec((orbitals, orbitals), lambda i: (0, 0))
    out = (part, length // count, orbitals)
    results = pl.pallas_call(
        functools.partial(x_kernel, count, group),
        grid=(part // group,),
        in_specs=[spec(*piece) for piece in pieces]
        + [
            pl.BlockSpec((1, length, group), lambda i: (i + first // group, 0, 0)),
            pl.BlockSpec((length, length), lambda i: (0, 0)),
            square,
        ],
        out_specs=[pl.BlockSpec((group,) + out[1:], lambda i: (i, 0, 0))] * count + [square],
        out_shape=[jax.ShapeDtypeStruct(out, jnp.bfloat16)] * count
        + [jax.ShapeDtypeStruct((orbitals, orbitals), jnp.float32)],
        **settings(),
    )(*[array for array, _ in pieces], fields, kinetic_x, gram)
    return results[:count], results[count]


def times_inverse(piece, inverse, turned, out):
    part, rows, _ = piece.shape
    product = jnp.dot(
        piece[...].reshape(part * rows, piece.shape[2]),
        inverse[...],
        preferred_element_type=jnp.float32,
    )
    for h in range(turned.shape[0]):
        for y in range(part):
            lines = product[y * rows : (y + 1) * rows, h * LANES : (h + 1) * LANES]
            turned[h, pl.ds(y * (rows + PAD), rows), :] = lines
        for r in range(rows):
            line = turned[h, pl.ds(r, part, stride=rows + PAD), :]
            out[r, :, h * LANES : (h + 1) * LANES] = line.astype(out.dtype)


def last_kernel(where, piece, inverse, *rest):
    times_inverse(piece, inverse, rest[-1], rest[-2])


def split_kernel(piece, inverse, *rest):
    for k, out in enumerate(rest[:-1]):
        pl.when(pl.program_id(0) == k)(
            functools.partial(times_inverse, piece, inverse, rest[-1], out)
        )


def place_kernel(where, piece, result, out):
    out[...] = piece[...]


def split(piece, inverse):
    part, lines, orbitals = piece.shape
    rows = 4 * ROWS if lines % (4 * ROWS) == 0 else lines
    out = (rows, part, orbitals)
    return pl.pallas_call(
        split_kernel,
        grid=(lines // rows,),
        in_specs=[
            pl.BlockSpec((part, rows, orbitals), lambda i: (0, i, 0)),
            pl.BlockSpec((orbitals, orbitals), lambda i: (0, 0)),
        ],
        out_specs=[pl.BlockSpec(out, lambda i: (0, 0, 0))] * (lines // rows),
        out_shape=[jax.ShapeDtypeStruct(out, jnp.bfloat16)] * (lines // rows),
        scratch_shapes=[pltpu.VMEM((orbitals // LANES, (part + 1) * (rows + PAD), LANES), jnp.float32)],
        **settings(VMEM_LEAST),
    )(piece, inverse)


def place(result, piece, begin, where):
    lines, part, orbitals = piece.shape
    rows = lines // 2 if begin % (lines // 2) == 0 else lines
    block = (rows, part, orbitals)
    return pl.pallas_call(
        place_kernel,
        grid_spec=pltpu.PrefetchScalarGridSpec(
            num_scalar_prefetch=1,
            grid=(lines // rows,),
            in_specs=[
                pl.BlockSpec(block, lambda i, where: (i, 0, 0)),
                pl.BlockSpec(memory_space=pl.ANY),
            ],
            out_specs=pl.BlockSpec(block, lambda i, where: (begin // rows + i, where[0], 0)),
        ),
        out_shape=jax.ShapeDtypeStruct(result.shape, result.dtype),
        input_output_aliases={2: 0},
        **settings(VMEM_LEAST),
    )(where.reshape(1), piece, result)


def finish(result, piece, inverse, place, width):
    part, lines, orbitals = piece.shape
    begun = result is not None
    rows = 4 * ROWS if lines % (4 * ROWS) == 0 else ROWS
    return pl.pallas_call(
        last_kernel,
        grid_spec=pltpu.PrefetchScalarGridSpec(
            num_scalar_prefetch=1,
            grid=(lines // rows,),
            in_specs=[
                pl.BlockSpec((part, rows, orbitals), lambda i, where: (0, i, 0)),
                pl.BlockSpec((orbitals, orbitals), lambda i, where: (0, 0)),
            ]
            + [pl.BlockSpec(memory_space=pl.ANY)] * begun,
            out_specs=pl.BlockSpec((rows, part, orbitals), lambda i, where: (i, where[0], 0)),
            scratch_shapes=[pltpu.VMEM((orbitals // LANES, (part + 1) * (rows + PAD), LANES), jnp.float32)],
        ),
        out_shape=jax.ShapeDtypeStruct((lines, width, orbitals), jnp.bfloat16),
        input_output_aliases={3: 0} if begun else {},
        **settings(VMEM_LEAST),
    )(place.reshape(1), piece, inverse, *([result] if begun else []))


def factor_kernel(scale, first, second, lower, inverse, work, upper):
    size = lower.shape[0]
    quarter = size // 4
    upper[3 * quarter :, :] = first[:, :size]
    upper[:quarter, :quarter] = first[:, size:]
    upper[2 * quarter : 3 * quarter, : 3 * quarter] = second[:, : 3 * quarter]
    upper[quarter : 2 * quarter, : 2 * quarter] = second[:, 3 * quarter :]
    row = lax.broadcasted_iota(jnp.int32, (size, size), 0)
    column = lax.broadcasted_iota(jnp.int32, (size, size), 1)
    work[:, :size] = jnp.where(row >= column, upper[...], upper[...].T) * scale
    work[:, size:] = jnp.where(row == column, 1.0, 0.0)
    line = lax.broadcasted_iota(jnp.int32, (BLOCK, 2 * BLOCK), 0)
    lane = lax.broadcasted_iota(jnp.int32, (BLOCK, 2 * BLOCK), 1)
    identity = jnp.where(lane == line, 1.0, 0.0)[:, :BLOCK]
    dot = functools.partial(
        jnp.dot, precision=lax.Precision.HIGHEST, preferred_element_type=jnp.float32
    )
    for begin in range(0, size, BLOCK):
        end = begin + BLOCK
        both = jnp.concatenate([work[begin:end, begin:end], identity], axis=1)
        for j in range(BLOCK):
            pivot_column = jnp.broadcast_to(both[:, j : j + 1], both.shape)
            pivot = jnp.broadcast_to(pivot_column[j : j + 1], both.shape)
            root = lax.rsqrt(pivot)
            root = root * (1.5 - 0.5 * pivot * root * root)
            pivot_row = jnp.broadcast_to(both[j : j + 1], both.shape) * root
            below = both - pivot_column * root * pivot_row
            both = jnp.where(line > j, below, jnp.where(line == j, pivot_row, both))
        panel = dot(both[:, BLOCK:], work[begin:end, :])
        upper[begin:end, :] = panel[:, :size]
        work[begin:end, size:] = panel[:, size:]
        if end < size:
            work[end:, :] -= dot(panel[:, end:size].T, panel)
    lower[...] = jnp.where(row >= column, upper[...].T, 0.0)
    inverse[...] = work[:, size:].T.astype(inverse.dtype)


def pack(gram):
    quarter = gram.shape[0] // 4
    first = [gram[3 * quarter :], gram[:quarter, :quarter]]
    second = [gram[2 * quarter : 3 * quarter, : 3 * quarter], gram[quarter : 2 * quarter, : 2 * quarter]]
    return jnp.concatenate(first, axis=1), jnp.concatenate(second, axis=1)


def factor(first, second, scale):
    size = first.shape[0] * 4
    return pl.pallas_call(
        functools.partial(factor_kernel, scale),
        out_shape=[
            jax.ShapeDtypeStruct((size, size), jnp.float32),
            jax.ShapeDtypeStruct((size, size), jnp.bfloat16),
        ],
        scratch_shapes=[
            pltpu.VMEM((size, 2 * size), jnp.float32),
            pltpu.VMEM((size, size), jnp.float32),
        ],
        **settings(VMEM_LEAST),
    )(first, second)


def one_determinant(walkers, fields, kinetic_x, kinetic_y, count):
    lines, width, orbitals = walkers.shape
    me = lax.axis_index("site")
    band = width // count
    part = ROWS if band % ROWS == 0 else band
    chunks = band // part
    group = 8 if part % 8 == 0 else part
    wide = 2 * part if band % (2 * part) == 0 else band
    steps = range(count)
    order = jnp.stack([partner(me, s, count) for s in steps])

    extra = rows_for_fields(lines, band, orbitals)
    far = [s for s in steps if s > 1 and lines > ROWS]
    near = [s for s in steps if s not in far]
    head = {}
    if far:
        cuts = [(s, 0, band) for s in far]
        arrays = apply_y(walkers, kinetic_y, fields, count, cuts, [ROWS] * len(far), far)
        kinetic_y, *arrays = tie(kinetic_y, *arrays)
        head = {s: trade(a, s, count) for s, a in zip(far, arrays)}
    near_cuts = [(0, part), (part, part), (2 * part, band - 2 * part)] if chunks >= 4 else [(0, band)]
    cuts = [(s, first, wide) for first in range(0, band, wide) for s in far]
    cuts += [(s, *cut) for s in near for cut in ([(0, band)] if s == 0 or not far else near_cuts)]
    sizes = [lines if s in near else lines - ROWS for s, _, _ in cuts]
    arrays = apply_y(walkers, kinetic_y, fields, count, cuts, sizes, near)
    tail = {(s, first): a for (s, first, _), a in zip(cuts, arrays)}
    def hold(key, *keys):
        held = tie(tail[key], *[tail[k] if isinstance(k, tuple) else head[k] for k in keys])
        tail[key] = held[0]
        for k, array in zip(keys, held[1:]):
            (tail if isinstance(k, tuple) else head)[k] = array

    sent = set()

    def go(key):
        tail[key] = trade(tail[key], key[0], count)
        sent.add(key)

    for s in far:
        go((s, 0))
    if far and chunks >= 4:
        y, z = (near[-1], 0), (near[-1], part)
        hold(y, *far)
        go(y)
        hold(z, y, *[(s, 0) for s in far])
        go(z)
    for key in tail:
        if key not in sent:
            go(key)
    own_fields = []
    for s in steps:
        sent = (head[s] if s in far else tail[s, 0])[-extra:, :ROWS]
        sent = sent.reshape(extra, ROWS, orbitals // band, band)
        own_fields.append(jnp.swapaxes(sent, 1, 2).reshape(-1, band)[:lines])
    own_fields = jnp.stack(own_fields)
    own_fields = own_fields.reshape(count * lines, band // group, group).swapaxes(0, 1)
    turned_x = kinetic_x.reshape(count, lines, count, lines)
    turned_x = jnp.take(jnp.take(turned_x, order, axis=0), order, axis=2).reshape(kinetic_x.shape)

    gram = jnp.zeros((orbitals, orbitals), jnp.float32)
    ready = []
    for first in range(0, band, part):
        pieces = []
        for s in steps:
            if s in far:
                pieces.append((head[s], 0))
            begin = max(at for step, at in tail if step == s and at <= first)
            pieces.append((tail[s, begin], begin))
        scaled, gram = apply_x(pieces, own_fields, turned_x, gram, count, first, part)
        ready.append(scaled)

    back = []
    for c in range(min(2, len(ready))):
        back.append(dict(enumerate(ready[c])))
        for s in far:
            if c == 1 and (s, wide) in tail:
                back[c][s], tail[s, wide] = tie(back[c][s], tail[s, wide])
            if c == 1 and s != far[0]:
                back[c][s], back[0][far[-1]] = tie(back[c][s], back[0][far[-1]])
            back[c][s] = trade(back[c][s], s, count)
    if count & (count - 1) == 0 and count > 1:
        core = me & 1
        if far:
            gram, back[0][far[0]] = tie(gram, back[0][far[0]])
        first, second = pack(gram)
        mine = jnp.where(core == 0, first, second)
        mine = mine + trade(jnp.where(core == 0, second, first), 1, count)
        step = 2
        while step < count:
            mine = mine + trade(mine, step, count)
            step *= 2
        if len(back) > 1 and far:
            mine, back[1][far[0]] = tie(mine, back[1][far[0]])
        other = trade(mine, 1, count)
        first, second = jnp.where(core == 0, mine, other), jnp.where(core == 0, other, mine)
    else:
        first, second = pack(lax.psum(gram, "site"))
    lower, inverse = factor(first, second, 1.0 / (count * lines * width))

    for c in range(2, len(ready)):
        back.append(dict(enumerate(ready[c])))
        for s in far:
            if c == 2:
                back[c][s], back[0][s] = tie(back[c][s], back[0][s])
            elif c < chunks - 1:
                back[c][s], inverse = tie(back[c][s], inverse)
            if 2 < c == chunks - 1:
                back[c][s] = [trade(piece, s, count) for piece in split(back[c][s], inverse)]
            else:
                back[c][s] = trade(back[c][s], s, count)
    for c in range(len(back)):
        for s in near:
            back[c][s], first = tie(back[c][s], first)
            back[c][s] = trade(back[c][s], s, count)

    result = None
    for c in range(chunks):
        for s in steps:
            if not isinstance(back[c][s], list):
                where = order[s] * chunks + c
                result = finish(result, back[c][s], inverse, where, width)
    for s in far:
        if isinstance(back[-1][s], list):
            pieces = back[-1][s]
            for k, piece in enumerate(pieces):
                where = order[s] * chunks + chunks - 1
                result = place(result, piece, k * piece.shape[0], where)
    return result, lower


def per_device(count, walkers, fields, kinetic_x, kinetic_y):
    results = [
        one_determinant(walkers[i], fields[i, 0], kinetic_x, kinetic_y, count)
        for i in range(walkers.shape[0])
    ]
    return tuple(jnp.stack(part) for part in zip(*results))


def solution(mesh):
    placed = (
        P(("grp", "spin"), "site", None, None),
        P(("grp", "spin"), None, "site", None),
        P(),
        P(),
    )
    return jax.shard_map(
        functools.partial(per_device, mesh.shape["site"]),
        mesh=mesh,
        in_specs=placed,
        out_specs=(P(("grp", "spin"), "site", None, None), P(("grp", "spin"), None, None)),
        check_vma=False,
    )
```
